256 devices in a mesh: ctx: 32 (over z, y_lo, core), tr: 2 (over y_hi), tc: 4 (over x).
Axes of the slice: x: 4, y: 4 (y_hi: 2, y_lo: 2; y = y_hi * 2 + y_lo), z: 8, core: 2. Of those that a mesh axis runs over, the one named last changes fastest.
Arguments:
- hidden: bfloat16 [16384, 4096], P(('ctx', 'tc'), 'tr'), may hold values from -6 to 6
- norm_gain: float32 [4096], P('tr'), may hold values from 0.25 to 1.75
- seg_lengths: int32 [64], replicated, may hold values from 1 to 512, 16384 in all
- q_weight: bfloat16 [4096, 2048], P('tr', 'tc'), may hold values from -3 to 3
- key_matrix: bfloat16 [4096, 512], P('tr', 'tc'), may hold values from -3 to 3
- value_matrix: bfloat16 [4096, 512], P('tr', 'tc'), may hold values from -0.09375 to 0.09375
- o_weight: bfloat16 [2048, 4096], P('tc', 'tr'), may hold values from -0.125 to 0.125
Outputs:
- layer_out: bfloat16 [16384, 4096], P(('ctx', 'tc'), 'tr')
The draws below stay inside these ranges and needn't reach their ends.
Inputs may be any that keep to these rules, and one draw needn't show every extreme that they name: `seg_lengths`: entry 0 is the length of the shared prefix, the other entries the candidates' lengths in list order; all sum to 16384, and the longest is exactly 512.
All inputs are finite; a program needn't handle non-finite values.
Results may differ from the reference program's by a relative error of at most 0.01.
Values may be sent and summed in bfloat16 or wider, within the bound.
No kernel may reach another device: no remote copies, remote signals or barrier semaphores. Data moves between devices by JAX's collectives and lax.ppermute only.
A program may use at most 64 MiB of HBM per device.

```python
import math
import jax
import jax.numpy as jnp
import numpy as np
from jax import lax

D = 4096
HEAD_SIZE = 128
QUERY_HEADS = 16
KEY_VALUE_HEADS = 4
TOK_DEV = 512
QW = 2048
KW = 512
SEQ = 16384
NSEG = 64
N_TR = 2


def feature_rank(key):
    order = jax.random.permutation(jax.random.fold_in(key, 101), D).astype(jnp.int32)
    rank = jnp.zeros((D,), jnp.int32).at[order].set(jnp.arange(D, dtype=jnp.int32))
    return (order, rank)


def inserted_weight(key, width, salt):
    order, rank = feature_rank(key)
    in_set = rank < D // 8
    base = jnp.clip(jax.random.normal(jax.random.fold_in(key, salt), (D, width), jnp.float32), -4.0, 4.0) * D ** (-0.5)
    column = jnp.arange(width, dtype=jnp.int32) % HEAD_SIZE == HEAD_SIZE // 2 - 1
    amplitude = math.sqrt(280.0 * math.sqrt(HEAD_SIZE)) / (2.121 * (D // 8))
    jitter = jax.random.uniform(jax.random.fold_in(key, salt + 1), (D, width), jnp.float32, 0.9, 1.1)
    planted = jnp.where(in_set[:, None], amplitude * jitter, 0.1 * base)
    return jnp.where(column[None, :], planted, base).astype(jnp.bfloat16)


def draw_q_weight(key, part):
    return inserted_weight(key, QUERY_HEADS * HEAD_SIZE, 7)


def draw_key_matrix(key, part):
    return inserted_weight(key, KEY_VALUE_HEADS * HEAD_SIZE, 17)


def rising_scale(low_end, high_end):
    fraction = jnp.arange(D, dtype=jnp.float32) / float(D - 1)
    return low_end + (high_end - low_end) * fraction


def draw_hidden(key, part):
    order, rank = feature_rank(key)
    count_set = D // 8
    in_set = rank < count_set
    row_block = min(256, SEQ)
    pairs = SEQ // row_block
    rows = jnp.clip(jax.random.normal(jax.random.fold_in(key, 4), (SEQ, D), jnp.float32), -3.3, 3.3)
    drawn = jnp.clip(jax.random.normal(jax.random.fold_in(key, 5), (pairs, D), jnp.float32), -3.3, 3.3)
    column_scale = rising_scale(0.6, 1.8)
    rows = rows * column_scale[None, :]
    drawn = drawn * column_scale[None, :]
    small = 0.01 * jnp.clip(jax.random.normal(jax.random.fold_in(key, 6), (SEQ, D), jnp.float32), -4.0, 4.0)
    rows = jnp.where(in_set[None, :], small, rows)
    strength = jax.random.uniform(jax.random.fold_in(key, 7), (pairs, 1), jnp.float32, 0.6, 1.0)
    planted_value = 3.0 * strength
    permuted = drawn[:, order]
    moved = jnp.concatenate([permuted[:, :count_set], jnp.roll(permuted[:, count_set:], 1, axis=1)], axis=1)
    partner = moved[:, rank]
    first = jnp.where(in_set[None, :], planted_value, drawn)
    second = jnp.where(in_set[None, :], planted_value * 1.01, partner)
    offsets = jax.random.randint(jax.random.fold_in(key, 8), (pairs,), 0, row_block - 1).astype(jnp.int32)
    starts = jnp.arange(pairs, dtype=jnp.int32) * row_block + offsets
    rows = rows.at[starts].set(first).at[starts + 1].set(second)
    return rows.astype(jnp.bfloat16)


def steps_of(stream_key, extent, pieces, smallest, high):
    factor_of, own = 1.0, jax.random.fold_in(stream_key, 6)
    for dim, parts in pieces:
        steps = jnp.exp(jax.random.uniform(jax.random.fold_in(own, dim), (parts,), jnp.float32, smallest / len(pieces), high / len(pieces)))
        factor_of = factor_of * jnp.repeat(steps, extent[dim] // parts).reshape([-1 if axis == dim else 1 for axis in range(len(extent))])
    return factor_of


def length_profile(count, total, bound, lean):
    weights = [(1 << 20) // math.isqrt(rank ** lean) + 1 for rank in range(2, count + 1)]
    surplus, counts = total - bound - (count - 1), [1] * (count - 1)
    while surplus > 0:
        movable = [i for i in range(count - 1) if counts[i] < bound]
        pool, budget = sum([weights[i] for i in movable]), surplus
        for i in movable:
            extra = min(bound - counts[i], max(1, budget * weights[i] // pool), surplus)
            counts[i] = counts[i] + extra
            surplus = surplus - extra
    return np.array([bound] + counts)


def uneven(own_key, amount, total, most, lean):
    if amount == 2:
        one = jax.random.randint(own_key, (), max(1, total - most), min(most, total - 1) + 1)
        return jnp.stack([one, total - one])
    lengths = jnp.asarray(length_profile(amount, total, most, lean), jnp.int32)
    couples = (amount - 1) // 2
    source_of, sink = lengths[1:1 + 2 * couples:2], lengths[2:2 + 2 * couples:2]
    margin = jnp.minimum(source_of - 1, most - sink)
    shifted = jax.random.randint(jax.random.fold_in(own_key, 1), (couples,), 0, 1 << 20) % (margin + 1)
    lengths = lengths.at[1:1 + 2 * couples:2].set(source_of - shifted).at[2:2 + 2 * couples:2].set(sink + shifted)
    return lengths[jax.random.permutation(jax.random.fold_in(own_key, 2), amount)]


def normal_values(own_key, shape, deviation, limit, pieces=(), held_as=jnp.bfloat16):
    result = jax.random.normal(own_key, shape, jnp.float32) * deviation
    if len(pieces) > 0:
        result = steps_of(own_key, shape, pieces, -0.22, 0.18) * result
    return jnp.clip(result, min=-limit, max=limit).astype(held_as)


def setup_inputs(seed: int = 0) -> dict:
    key_list = jax.random.split(jax.random.key(seed), 8)
    return {
        "hidden": draw_hidden(jax.random.fold_in(key_list[7], 71), 0),
        "norm_gain": jnp.clip(1.0 + 0.15 * jax.random.normal(key_list[1], (D,), jnp.float32), 0.25, 1.75),
        "seg_lengths": uneven(key_list[2], NSEG, SEQ, TOK_DEV, 1).astype(jnp.int32),
        "q_weight": draw_q_weight(jax.random.fold_in(key_list[7], 71), 0),
        "key_matrix": draw_key_matrix(jax.random.fold_in(key_list[7], 71), 0),
        "value_matrix": normal_values(key_list[5], (D, KW), D ** -0.5, 0.09375, ((0, 2), (1, 4))),
        "o_weight": normal_values(key_list[6], (QW, D), QW ** -0.5, 0.125, ((0, 4), (1, 2))),
    }


epsilon = 1e-05
rope_base = 500000.0
masked_score = -1e+30

def rotate(heads_data, positions):
    half_dim = heads_data.shape[-1] // 2
    frequency = rope_base ** (-(jnp.arange(half_dim, dtype=jnp.float32) * 2.0 / heads_data.shape[-1]))
    angles = positions.astype(jnp.float32)[:, None] * frequency[None, :]
    cosine = jnp.cos(angles)[:, None, :]
    sine_part = jnp.sin(angles)[:, None, :]
    first = heads_data[..., :half_dim]
    second = heads_data[..., half_dim:]
    return jnp.concatenate([first * cosine - second * sine_part, second * cosine + first * sine_part], axis=-1)

def segment_of(positions, seg_lengths):
    bounds = jnp.cumsum(seg_lengths)[:-1]
    return lax.optimization_barrier(jnp.sum((positions[:, None] >= bounds[None, :]).astype(jnp.int32), axis=1))

def reference(hidden, norm_gain, seg_lengths, q_weight, key_matrix, value_matrix, o_weight):
    count_of_tokens = hidden.shape[0]
    wide_hidden = hidden.astype(jnp.float32)
    power = lax.optimization_barrier(jnp.mean(wide_hidden * wide_hidden, axis=1, keepdims=True))
    normalized_rows = (wide_hidden * lax.rsqrt(power + epsilon) * norm_gain).astype(jnp.bfloat16)
    positions = jnp.arange(count_of_tokens, dtype=jnp.int32)
    queries = jnp.dot(normalized_rows, q_weight, preferred_element_type=jnp.float32).reshape(count_of_tokens, QUERY_HEADS, HEAD_SIZE)
    key_block_list = jnp.dot(normalized_rows, key_matrix, preferred_element_type=jnp.float32).reshape(count_of_tokens, KEY_VALUE_HEADS, HEAD_SIZE)
    value_block_list = jnp.dot(normalized_rows, value_matrix, preferred_element_type=jnp.float32).reshape(count_of_tokens, KEY_VALUE_HEADS, HEAD_SIZE)
    queries = rotate(queries, positions).astype(jnp.bfloat16)
    key_block_list = rotate(key_block_list, positions).astype(jnp.bfloat16)
    value_block_list = value_block_list.astype(jnp.bfloat16)
    segments = segment_of(positions, seg_lengths)
    rows_per_block = TOK_DEV // N_TR
    head_groups = QUERY_HEADS // KEY_VALUE_HEADS
    wide_keys = key_block_list.astype(jnp.float32)
    wide_values = value_block_list.astype(jnp.float32)
    score_scale = HEAD_SIZE ** (-0.5)

    def one_block(block_index):
        block_start = block_index * rows_per_block
        block_queries = lax.dynamic_slice_in_dim(queries, block_start, rows_per_block, 0)
        block_queries = block_queries.astype(jnp.float32).reshape(rows_per_block, KEY_VALUE_HEADS, head_groups, HEAD_SIZE)
        query_pos = block_start + jnp.arange(rows_per_block, dtype=jnp.int32)
        query_seg = lax.dynamic_slice_in_dim(segments, block_start, rows_per_block, 0)
        visible = (positions[None, :] <= query_pos[:, None]) & ((segments[None, :] == 0) | (segments[None, :] == query_seg[:, None]))
        scores = jnp.einsum('qhgd,khd->hgqk', block_queries, wide_keys) * score_scale
        scores = jnp.where(visible, scores, masked_score)
        largest = lax.optimization_barrier(jnp.max(scores, axis=-1, keepdims=True))
        weights = jnp.where(visible, jnp.exp(scores - largest), 0.0)
        weight_sum = lax.optimization_barrier(jnp.sum(weights, axis=-1))
        rounded = lax.optimization_barrier(weights.astype(jnp.bfloat16)).astype(jnp.float32)
        mixed = jnp.einsum('hgqk,khd->hgqd', rounded, wide_values) / weight_sum[..., None]
        return jnp.transpose(mixed, (2, 0, 1, 3)).reshape(rows_per_block, QUERY_HEADS * HEAD_SIZE).astype(jnp.bfloat16)
    blocks = lax.map(one_block, jnp.arange(count_of_tokens // rows_per_block, dtype=jnp.int32))
    attended = blocks.reshape(count_of_tokens, QUERY_HEADS * HEAD_SIZE)
    projected = jnp.dot(attended, o_weight, preferred_element_type=jnp.float32)
    return (wide_hidden + projected).astype(jnp.bfloat16)
```

```python
import functools

import jax
import jax.numpy as jnp
from jax import lax
from jax.experimental import pallas as pl
from jax.experimental.pallas import tpu as pltpu
from jax.sharding import PartitionSpec as P

D = 4096
HEAD = 128
HALF = HEAD // 2
EPS = 1e-05
ROPE_BASE = 500000.0
MASKED = -1e30
ROWS = 128
HEADS = 4
QW = HEADS * HEAD
BLOCK = 512
SCALE = HEAD ** (-0.5)
LOG2E = 1.4426950408889634

f32 = jnp.float32
bf16 = jnp.bfloat16


def spec(memory=pltpu.VMEM):
    return pl.BlockSpec(memory_space=memory)


def rel(x, axis, n, distance):
    return lax.ppermute(x, axis, [((i + distance) % n, i) for i in range(n)])


def qkv_kernel(first, count, *refs):
    idx_ref, power_ref, gain_ref, wq_ref, wk_ref, wv_ref = refs[:6]
    h_refs = refs[6 : 6 + count]
    keep_refs = refs[6 + count : 6 + 2 * count]
    send_refs = refs[6 + 2 * count :]
    tc = idx_ref[0]
    row = lax.broadcasted_iota(jnp.int32, (ROWS, ROWS), 0)
    col = lax.broadcasted_iota(jnp.int32, (ROWS, ROWS), 1)
    gain = gain_ref[...]
    parts = []
    for n in range(count):
        rows = power_ref[pl.ds((tc + first[n]) % 4, 1), :]
        column = jnp.sum(jnp.where(row == col, rows, 0.0), axis=1, keepdims=True)
        scale = lax.rsqrt(column / D + EPS)
        parts.append((h_refs[n][...].astype(f32) * scale * gain).astype(bf16))
    x = parts[0] if count == 1 else jnp.concatenate(parts, axis=0)
    q = jnp.dot(x, wq_ref[...], preferred_element_type=f32)
    k = jnp.dot(x, wk_ref[...], preferred_element_type=f32)
    v = jnp.dot(x, wv_ref[...], preferred_element_type=f32)
    high = k.astype(bf16)
    low = (k - high.astype(f32)).astype(bf16)
    for n in range(count):
        s = slice(n * ROWS, (n + 1) * ROWS)
        keep_refs[n][:, :QW] = q[s]
        keep_refs[n][:, QW : QW + HEAD] = k[s]
        keep_refs[n][:, QW + HEAD :] = v[s]
        send_refs[n][:, :QW] = q[s].astype(bf16)
        send_refs[n][:, QW : QW + HEAD] = v[s].astype(bf16)
        send_refs[n][:, QW + HEAD : QW + 2 * HEAD] = high[s]
        send_refs[n][:, QW + 2 * HEAD :] = low[s]


def qkv(chunks, idx, power, gain, wq, wk, wv, hs):
    n = len(chunks)
    keep = jax.ShapeDtypeStruct((ROWS, QW + 2 * HEAD), f32)
    send = jax.ShapeDtypeStruct((ROWS, QW + 3 * HEAD), bf16)
    out = pl.pallas_call(
        functools.partial(qkv_kernel, chunks, n),
        out_shape=[keep] * n + [send] * n,
        in_specs=[spec(pltpu.SMEM)] + [spec()] * (5 + n),
        out_specs=[spec()] * (2 * n),
        compiler_params=pltpu.CompilerParams(vmem_limit_bytes=24 << 20),
        cost_estimate=pl.CostEstimate(
            flops=2 * n * ROWS * 2048 * 768, bytes_accessed=4 << 20, transcendentals=0
        ),
        name="qkv",
    )(idx, power, gain, wq, wk, wv, *hs)
    return out[:n], out[n:]


def rotated(u, cosine, sine):
    first, second = u[:, :HALF], u[:, HALF:]
    return jnp.concatenate(
        [first * cosine - second * sine, second * cosine + first * sine], axis=1
    )


def rotary_kernel(*refs):
    keep_refs, got_refs = refs[:4], refs[4:8]
    cos_ref, sin_ref, q_ref, kv_ref = refs[8:]
    for r in range(4):
        s = slice(r * ROWS, (r + 1) * ROWS)
        cosine, sine = cos_ref[s, :], sin_ref[s, :]
        keep, got = keep_refs[r], got_refs[r]
        for h in range(HEADS):
            c = slice(h * HEAD, (h + 1) * HEAD)
            u = keep[:, c] + got[:, c].astype(f32)
            q_ref[s, c] = rotated(u, cosine, sine).astype(bf16)
        k = keep[:, QW : QW + HEAD] + (
            got[:, QW + HEAD : QW + 2 * HEAD].astype(f32) + got[:, QW + 2 * HEAD :].astype(f32)
        )
        kv_ref[s, :HEAD] = rotated(k, cosine, sine).astype(bf16)
        v = keep[:, QW + HEAD :] + got[:, QW : QW + HEAD].astype(f32)
        kv_ref[s, HEAD:] = v.astype(bf16)


def rotary(keeps, gots, cosine, sine):
    return pl.pallas_call(
        rotary_kernel,
        out_shape=[
            jax.ShapeDtypeStruct((BLOCK, QW), bf16),
            jax.ShapeDtypeStruct((BLOCK, 2 * HEAD), bf16),
        ],
        in_specs=[spec()] * 10,
        out_specs=[spec()] * 2,
        compiler_params=pltpu.CompilerParams(vmem_limit_bytes=16 << 20),
        cost_estimate=pl.CostEstimate(flops=8 << 20, bytes_accessed=4 << 20, transcendentals=0),
        name="rotary",
    )(*keeps, *gots, cosine, sine)


def attend_kernel(r, idx_ref, len_ref, q_ref, own_ref, prev_ref, pre_a_ref, pre_b_ref, wo_ref, out_ref, bias_ref):
    tc, ctx = idx_ref[0], idx_ref[1]
    a = (tc + r) % 4
    base = ctx * BLOCK + a * ROWS
    lengths = len_ref[...]
    i = lax.broadcasted_iota(jnp.int32, (64, 64), 0)
    j = lax.broadcasted_iota(jnp.int32, (64, 64), 1)
    starts = jnp.sum(jnp.where(i < j, lengths.astype(f32), 0.0), axis=0, keepdims=True)
    pos = base + lax.broadcasted_iota(jnp.int32, (ROWS, 64), 0)
    begun = jnp.where(starts <= pos.astype(f32), starts, 0.0)
    start = jnp.max(begun, axis=1, keepdims=True).astype(jnp.int32)
    prefix = jnp.sum(jnp.where(i[:, :1] < 1, lengths, 0).astype(f32), axis=0, keepdims=True).astype(jnp.int32)
    t = base + lax.broadcasted_iota(jnp.int32, (ROWS, 1), 0)
    low = jnp.where(start >= prefix, start, jnp.int32(1 << 30))
    high = jnp.minimum(prefix, t + 1)
    lane = lax.broadcasted_iota(jnp.int32, (ROWS, ROWS), 1)
    keys, values = [], []
    for n in range(5):
        c = (r + n) % 4
        s = slice(c * ROWS, (c + 1) * ROWS)
        if n == 0:
            chunk = prev_ref[s, :]
        elif n == 4:
            chunk = own_ref[s, :]
        else:
            chunk = jnp.where(a + n < 4, prev_ref[s, :], own_ref[s, :])
        keys.append(chunk[:, :HEAD])
        values.append(chunk[:, HEAD:])
        u = base + (n - 4) * ROWS + lane
        seen = (u >= low) & (u <= t)
        bias_ref[:, n * ROWS : (n + 1) * ROWS] = jnp.where(seen, 0.0, MASKED)
    for c in range(4):
        s = slice(c * ROWS, (c + 1) * ROWS)
        chunk = pre_a_ref[s, :] + pre_b_ref[s, :]
        keys.append(chunk[:, :HEAD])
        values.append(chunk[:, HEAD:])
        u = ((tc + c) % 4) * ROWS + lane
        n = 5 + c
        bias_ref[:, n * ROWS : (n + 1) * ROWS] = jnp.where(u < high, 0.0, MASKED)
    keys = jnp.concatenate(keys, axis=0)
    values = jnp.concatenate(values, axis=0)
    outs = []
    for h in range(HEADS):
        q = q_ref[r * ROWS : (r + 1) * ROWS, h * HEAD : (h + 1) * HEAD]
        s = lax.dot_general(q, keys, (((1,), (1,)), ((), ())), preferred_element_type=f32)
        s = s + bias_ref[...]
        largest = jnp.max(s, axis=1, keepdims=True)
        p = jnp.exp2((s - largest) * (SCALE * LOG2E))
        total = jnp.sum(p, axis=1, keepdims=True)
        mixed = jnp.dot(p.astype(bf16), values, preferred_element_type=f32)
        outs.append((mixed / total).astype(bf16))
    attended = jnp.concatenate(outs, axis=1)
    out_ref[...] = jnp.dot(attended, wo_ref[...], preferred_element_type=f32).astype(out_ref.dtype)


def attend(r, idx, lengths, q, own, prev, pre_a, pre_b, wo, dtype):
    return pl.pallas_call(
        functools.partial(attend_kernel, r),
        out_shape=jax.ShapeDtypeStruct((ROWS, 2048), dtype),
        in_specs=[spec(pltpu.SMEM)] + [spec()] * 7,
        out_specs=spec(),
        scratch_shapes=[pltpu.VMEM((ROWS, 9 * ROWS), f32)],
        compiler_params=pltpu.CompilerParams(vmem_limit_bytes=24 << 20),
        cost_estimate=pl.CostEstimate(
            flops=4 * ROWS * QW * 1152 + 2 * ROWS * QW * 2048,
            bytes_accessed=4 << 20,
            transcendentals=4 * ROWS * 1152,
        ),
        name="attend",
    )(idx, lengths, q, own, prev, pre_a, pre_b, wo)


def ctx_send(x, pairs):
    return lax.ppermute(x, "ctx", pairs)


def per_device(hidden, norm_gain, seg_lengths, wq, wk, wv, wo):
    tc = lax.axis_index("tc")
    ctx = lax.axis_index("ctx")
    idx = jnp.stack([tc, ctx]).astype(jnp.int32)
    h2 = rel(hidden, "tc", 4, 2)
    h1 = rel(hidden, "tc", 4, 1)
    h3 = rel(hidden, "tc", 4, 3)
    wide = hidden.astype(f32)
    mine = jnp.sum(wide * wide, axis=1)
    placed = jnp.where(jnp.arange(4)[:, None] == tc, mine[None, :], 0.0)
    power = lax.psum(placed, ("tr", "tc"))
    gain = norm_gain.reshape(1, -1)
    offset = (jnp.arange(4, dtype=jnp.int32) + tc) % 4 * ROWS
    positions = (ctx * BLOCK + offset[:, None] + jnp.arange(ROWS, dtype=jnp.int32)[None, :]).reshape(-1)
    frequency = ROPE_BASE ** (-(jnp.arange(HALF, dtype=f32) * 2.0 / HEAD))
    angles = positions.astype(f32)[:, None] * frequency[None, :]
    cosine, sine = jnp.cos(angles), jnp.sin(angles)
    lengths = seg_lengths.reshape(-1, 1)

    keeps, gots = [None] * 4, [None] * 4
    for chunks, hs in (((0,), (hidden,)), ((1, 3), (h1, h3)), ((2,), (h2,))):
        kept, sent = qkv(chunks, idx, power, gain, wq, wk, wv, hs)
        for c, k, s in zip(chunks, kept, sent):
            keeps[c] = k
            gots[c] = rel(s, "tr", 2, 1)
    q, kv = rotary(keeps, gots, cosine, sine)
    prev = ctx_send(kv, [(i, i + 1) for i in range(31)])
    at = jnp.where(ctx == 0, kv, jnp.zeros_like(kv))
    got = [ctx_send(kv, [(0, 4 * z)]) for z in (2, 4, 6)]
    at = at + got[0] + got[1] + got[2]
    even = [0, 8, 16, 24]
    got = [ctx_send(at, [(e, e + d) for e in even]) for d in (4, 6, 2)]
    at = at + got[0] + got[1] + got[2]
    other = ctx_send(at, [(2 * i, 2 * i + 1) for i in range(16)])
    parts = {}
    for r in (2, 1, 3, 0):
        parts[r] = attend(r, idx, lengths, q, kv, prev, at, other, wo, f32 if r == 0 else bf16)
    total = parts[0]
    for r in (1, 3, 2):
        total = total + rel(parts[r], "tc", 4, -r).astype(f32)
    return (hidden.astype(f32) + total).astype(bf16)


def solution(mesh):
    in_specs = (
        P(("ctx", "tc"), "tr"),
        P("tr"),
        P(),
        P("tr", "tc"),
        P("tr", "tc"),
        P("tr", "tc"),
        P("tc", "tr"),
    )
    out_specs = P(("ctx", "tc"), "tr")
    return jax.shard_map(
        per_device, mesh=mesh, in_specs=in_specs, out_specs=out_specs, check_vma=False
    )
```

```python
import functools

import jax
import jax.numpy as jnp
from jax import lax
from jax.experimental import pallas as pl
from jax.experimental.pallas import tpu as pltpu
from jax.sharding import PartitionSpec as P

D = 4096
HEAD = 128
HALF = HEAD // 2
EPS = 1e-05
ROPE_BASE = 500000.0
MASKED = -1e30
ROWS = 128
HEADS = 4
QW = HEADS * HEAD
BLOCK = 512
SCALE = HEAD ** (-0.5)
EXPONENT = SCALE * 1.4426950408889634

f32 = jnp.float32
bf16 = jnp.bfloat16


def spec(memory=pltpu.VMEM):
    return pl.BlockSpec(memory_space=memory)


def rel(x, axis, n, distance):
    return lax.ppermute(x, axis, [((i + distance) % n, i) for i in range(n)])


def call(kernel, name, out_shape, ins, smem=0, stay=(), scratch=(), vmem=24, flops=0, exps=0):
    many = isinstance(out_shape, list)
    where = [pltpu.SMEM] * smem + [pltpu.HBM if n in stay else pltpu.VMEM for n in range(smem, len(ins))]
    return pl.pallas_call(
        kernel,
        out_shape=out_shape,
        in_specs=[spec(w) for w in where],
        out_specs=[spec()] * len(out_shape) if many else spec(),
        scratch_shapes=list(scratch),
        compiler_params=pltpu.CompilerParams(vmem_limit_bytes=vmem << 20),
        cost_estimate=pl.CostEstimate(flops=flops, bytes_accessed=4 << 20, transcendentals=exps),
        name=name,
    )(*ins)


def square_column(n):
    return lax.broadcasted_iota(jnp.int32, (n, n), 0) == lax.broadcasted_iota(jnp.int32, (n, n), 1)


def fetch(sems, *pairs):
    copies = [pltpu.make_async_copy(src, dst, sems.at[n]) for n, (src, dst) in enumerate(pairs)]
    for copy in copies:
        copy.start()
    return copies


def squares_kernel(h_ref, out_ref, held, sems):
    fetch(sems, (h_ref, held))[0].wait()
    h = held[...].astype(f32)
    column = jnp.sum(h * h, axis=1, keepdims=True)
    row = jnp.sum(jnp.where(square_column(ROWS), column, 0.0), axis=0, keepdims=True)
    out_ref[...] = jnp.broadcast_to(row, (8, ROWS))


def normed(h, power, gain):
    column = jnp.sum(jnp.where(square_column(ROWS), power, 0.0), axis=1, keepdims=True)
    return (h.astype(f32) * lax.rsqrt(column / D + EPS) * gain).astype(bf16)


def put_kv(x, wk_ref, wv_ref, keep_ref, send_ref):
    k = jnp.dot(x, wk_ref[...], preferred_element_type=f32)
    v = jnp.dot(x, wv_ref[...], preferred_element_type=f32)
    high = k.astype(bf16)
    keep_ref[:, :HEAD] = v
    keep_ref[:, HEAD:] = k
    send_ref[:, :HEAD] = v.astype(bf16)
    send_ref[:, HEAD : 2 * HEAD] = high
    send_ref[:, 2 * HEAD : 3 * HEAD] = (k - high.astype(f32)).astype(bf16)


def put_q(x, wq_ref, keep_ref, send_ref, at):
    q = jnp.dot(x, wq_ref[...], preferred_element_type=f32)
    keep_ref[...] = q
    send_ref[:, at : at + QW] = q.astype(bf16)


def own_kernel(gain_ref, wq_ref, wk_ref, wv_ref, mine_ref, theirs_ref, h_ref, kv_ref, q_ref, send_ref, h, wq, wk, wv, sems):
    pending = fetch(sems, (h_ref, h), (wk_ref, wk), (wv_ref, wv), (wq_ref, wq))
    pending[0].wait()
    x = normed(h[...], mine_ref[:1, :] + theirs_ref[:1, :], gain_ref[...])
    pending[1].wait()
    pending[2].wait()
    put_kv(x, wk, wv, kv_ref, send_ref)
    pending[3].wait()
    put_q(x, wq, q_ref, send_ref, 3 * HEAD)


def others_kernel(n, gain_ref, wk_ref, wv_ref, *refs):
    powers, halves = refs[:n], refs[n : 3 * n]
    x_ref, kv_ref, send_ref, wk, wv, sems = refs[3 * n :]
    pending = fetch(sems, (wk_ref, wk), (wv_ref, wv))
    for c in range(n):
        h = jnp.concatenate([halves[2 * c][...], halves[2 * c + 1][...]], axis=0)
        x_ref[c * ROWS : (c + 1) * ROWS, :] = normed(h, powers[c][:1, :], gain_ref[...])
    for copy in pending:
        copy.wait()
    put_kv(x_ref[...], wk, wv, kv_ref, send_ref)


def q_kernel(xa_ref, xb_ref, wq_ref, keep_ref, send_ref, wq, sems):
    for copy in fetch(sems, (wq_ref, wq)):
        copy.wait()
    q = jnp.dot(jnp.concatenate([xa_ref[...], xb_ref[...]], axis=0), wq[...], preferred_element_type=f32)
    keep_ref[...] = q
    send_ref[...] = q.astype(bf16)


def rotated(u, cosine, sine):
    return (u * cosine + pltpu.roll(u, HALF, 1) * sine).astype(bf16)


def rotary_kv_kernel(keep0_ref, got0_ref, keepa_ref, gota_ref, keepb_ref, gotb_ref, cos_ref, sin_ref, kv_ref):
    for keep, got, s in (
        (keep0_ref, got0_ref, slice(0, ROWS)),
        (keepa_ref, gota_ref, slice(ROWS, 3 * ROWS)),
        (keepb_ref, gotb_ref, slice(3 * ROWS, BLOCK)),
    ):
        k = keep[:, HEAD:] + (
            got[:, HEAD : 2 * HEAD].astype(f32) + got[:, 2 * HEAD : 3 * HEAD].astype(f32)
        )
        kv_ref[s, :HEAD] = rotated(k, cos_ref[s, :], sin_ref[s, :])
        kv_ref[s, HEAD:] = (keep[:, :HEAD] + got[:, :HEAD].astype(f32)).astype(bf16)


def rotary_q_kernel(keep0_ref, got0_ref, keep_ref, got_ref, cos_ref, sin_ref, q_ref):
    for keep, got, s, at in (
        (keep0_ref, got0_ref, slice(0, ROWS), 3 * HEAD),
        (keep_ref, got_ref, slice(ROWS, BLOCK), 0),
    ):
        for h in range(HEADS):
            w = slice(h * HEAD, (h + 1) * HEAD)
            u = keep[:, w] + got[:, at + h * HEAD : at + (h + 1) * HEAD].astype(f32)
            q_ref[s, w] = rotated(u, cos_ref[s, :], sin_ref[s, :])


def chunk_of(ref, c):
    at = (0, 1, 3, 2)[c] * ROWS
    return ref[at : at + ROWS, :]


def stacked(q):
    return jnp.concatenate([q[:, h * HEAD : (h + 1) * HEAD] for h in range(HEADS)], axis=0)


def local_kernel(idx_ref, len_ref, q_ref, own_ref, prev_ref, acc_ref, max_ref, sum_ref, bias_ref):
    tc, ctx = idx_ref[0], idx_ref[1]
    lengths = len_ref[...].astype(f32)
    i = lax.broadcasted_iota(jnp.int32, (64, 64), 0)
    j = lax.broadcasted_iota(jnp.int32, (64, 64), 1)
    starts = jnp.sum(jnp.where(i < j, lengths, 0.0), axis=0, keepdims=True)
    prefix = jnp.sum(jnp.where(i[:, :1] < 1, lengths, 0.0), axis=0, keepdims=True).astype(jnp.int32)
    lane = lax.broadcasted_iota(jnp.int32, (ROWS, ROWS), 1)
    for r in range(4):
        a = (tc + r) % 4
        base = ctx * BLOCK + a * ROWS
        pos = base + lax.broadcasted_iota(jnp.int32, (ROWS, 64), 0)
        begun = jnp.where(starts <= pos.astype(f32), starts, 0.0)
        start = jnp.max(begun, axis=1, keepdims=True).astype(jnp.int32)
        t = base + lax.broadcasted_iota(jnp.int32, (ROWS, 1), 0)
        low = jnp.where(start >= prefix, start, jnp.int32(1 << 30))
        keys, values = [], []
        for n in range(5):
            c = (r + n) % 4
            if n == 0:
                chunk = chunk_of(prev_ref, c)
            elif n == 4:
                chunk = chunk_of(own_ref, c)
            else:
                chunk = jnp.where(a + n < 4, chunk_of(prev_ref, c), chunk_of(own_ref, c))
            keys.append(chunk[:, :HEAD])
            values.append(chunk[:, HEAD:])
            u = base + (n - 4) * ROWS + lane
            bias_ref[:, n * ROWS : (n + 1) * ROWS] = jnp.where((u >= low) & (u <= t), 0.0, MASKED)
        keys = jnp.concatenate(keys, axis=0)
        values = jnp.concatenate(values, axis=0)
        q = stacked(chunk_of(q_ref, r))
        s = lax.dot_general(q, keys, (((1,), (1,)), ((), ())), preferred_element_type=f32)
        s = (s.reshape(HEADS, ROWS, 5 * ROWS) + bias_ref[...][None]).reshape(BLOCK, 5 * ROWS)
        largest = jnp.max(s, axis=1, keepdims=True)
        p = jnp.exp2((s - largest) * EXPONENT)
        total = jnp.sum(p, axis=1, keepdims=True)
        acc_ref[r] = jnp.dot(p.astype(bf16), values, preferred_element_type=f32)
        max_ref[r] = jnp.broadcast_to(largest, (BLOCK, HEAD))
        sum_ref[r] = jnp.broadcast_to(total, (BLOCK, HEAD))


def local(idx, lengths, q, own, prev):
    shape = jax.ShapeDtypeStruct((4, BLOCK, HEAD), f32)
    return call(
        local_kernel, "local", [shape] * 3, (idx, lengths, q, own, prev), smem=1,
        scratch=[pltpu.VMEM((ROWS, 5 * ROWS), f32)], vmem=32,
        flops=4 * BLOCK * QW * 640, exps=4 * BLOCK * 640,
    )


def prefix_kernel(r, idx_ref, len_ref, acc_ref, max_ref, sum_ref, q_ref, pre_ref, other_ref, wo_ref, out_ref, bias_ref):
    tc, ctx = idx_ref[0], idx_ref[1]
    base = ctx * BLOCK + (tc + r) % 4 * ROWS
    lengths = len_ref[...].astype(f32)
    i = lax.broadcasted_iota(jnp.int32, (64, 1), 0)
    prefix = jnp.sum(jnp.where(i < 1, lengths, 0.0), axis=0, keepdims=True).astype(jnp.int32)
    high = jnp.minimum(prefix, base + 1 + lax.broadcasted_iota(jnp.int32, (ROWS, 1), 0))
    lane = lax.broadcasted_iota(jnp.int32, (ROWS, ROWS), 1)
    keys, values = [], []
    for c in range(4):
        chunk = chunk_of(pre_ref, c) + chunk_of(other_ref, c)
        keys.append(chunk[:, :HEAD])
        values.append(chunk[:, HEAD:])
        u = ((tc + c) % 4) * ROWS + lane
        bias_ref[:, c * ROWS : (c + 1) * ROWS] = jnp.where(u < high, 0.0, MASKED)
    keys = jnp.concatenate(keys, axis=0)
    values = jnp.concatenate(values, axis=0)
    q = stacked(chunk_of(q_ref, r))
    s = lax.dot_general(q, keys, (((1,), (1,)), ((), ())), preferred_element_type=f32)
    s = (s.reshape(HEADS, ROWS, BLOCK) + bias_ref[...][None]).reshape(BLOCK, BLOCK)
    before = max_ref[r][:, :1]
    largest = jnp.maximum(jnp.max(s, axis=1, keepdims=True), before)
    p = jnp.exp2((s - largest) * EXPONENT)
    factor = jnp.exp2((before - largest) * EXPONENT)
    total = jnp.sum(p, axis=1, keepdims=True) + factor * sum_ref[r][:, :1]
    mixed = jnp.dot(p.astype(bf16), values, preferred_element_type=f32) + factor * acc_ref[r]
    mixed = (mixed / total).astype(bf16)
    attended = jnp.concatenate([mixed[h * ROWS : (h + 1) * ROWS] for h in range(HEADS)], axis=1)
    out_ref[...] = jnp.dot(attended, wo_ref[...], preferred_element_type=f32).astype(out_ref.dtype)


def finish(r, idx, lengths, state, q, pre, wo, dtype):
    return call(
        functools.partial(prefix_kernel, r), "prefix", jax.ShapeDtypeStruct((ROWS, 2048), dtype),
        (idx, lengths, *state, q, *pre, wo), smem=1,
        scratch=[pltpu.VMEM((ROWS, BLOCK), f32)],
        flops=4 * ROWS * QW * 512 + 2 * ROWS * QW * 2048, exps=4 * ROWS * 512,
    )


def spread_far(x, ctx):
    at = jnp.where(ctx == 0, x, jnp.zeros_like(x))
    got = [lax.ppermute(x, "ctx", [(0, 4 * z)]) for z in (2, 4, 6)]
    at = at + got[0] + got[1] + got[2]
    return at, [lax.ppermute(at, "ctx", [(e, e + d) for e in (0, 8, 16, 24)]) for d in (4, 6, 2)]


def held(*arrays):
    return [pltpu.VMEM(a.shape, a.dtype) for a in arrays] + [pltpu.SemaphoreType.DMA((len(arrays),))]


def per_device(hidden, norm_gain, seg_lengths, wq, wk, wv, wo):
    tc = lax.axis_index("tc")
    ctx = lax.axis_index("ctx")
    idx = jnp.stack([tc, ctx]).astype(jnp.int32)
    upper, lower = hidden[:HALF], hidden[HALF:]
    h1u = rel(upper, "tc", 4, 1)
    h3l = rel(lower, "tc", 4, 3)
    h1l = rel(lower, "tc", 4, 1)
    h3u = rel(upper, "tc", 4, 3)
    h2u = rel(h1u, "tc", 4, 1)
    h2l = rel(h3l, "tc", 4, 3)
    mine = call(
        squares_kernel, "squares", jax.ShapeDtypeStruct((8, ROWS), f32), (hidden,), stay=(0,),
        scratch=held(hidden),
    )
    theirs = rel(mine, "tr", 2, 1)
    theirs, _, _ = lax.optimization_barrier((theirs, h1u, h3l))
    gain = norm_gain.reshape(1, -1)
    offset = (jnp.array([0, 1, 3, 2], jnp.int32) + tc) % 4 * ROWS
    positions = (ctx * BLOCK + offset[:, None] + jnp.arange(ROWS, dtype=jnp.int32)[None, :]).reshape(-1)
    frequency = ROPE_BASE ** (-(jnp.arange(HALF, dtype=f32) * 2.0 / HEAD))
    angles = positions.astype(f32)[:, None] * jnp.concatenate([frequency, frequency])[None, :]
    cosine = jnp.cos(angles)
    sine = jnp.sin(angles) * jnp.where(jnp.arange(HEAD) < HALF, -1.0, 1.0)[None, :]
    lengths = seg_lengths.reshape(-1, 1)

    def shape(rows, columns, dtype):
        return jax.ShapeDtypeStruct((rows, columns), dtype)

    kv0, q0, send0 = call(
        own_kernel, "own", [shape(ROWS, 2 * HEAD, f32), shape(ROWS, QW, f32), shape(ROWS, 7 * HEAD, bf16)],
        (gain, wq, wk, wv, mine, theirs, hidden), stay=(1, 2, 3, 6),
        scratch=held(hidden, wq, wk, wv), flops=2 * ROWS * 2048 * 768,
    )
    got0 = rel(send0, "tr", 2, 1)
    power, send0 = lax.optimization_barrier((mine + theirs, send0))
    p1, p3, p2 = [rel(power, "tc", 4, d) for d in (1, 3, 2)]

    def others(powers, hs):
        rows = ROWS * len(powers)
        return call(
            functools.partial(others_kernel, len(powers)), "others",
            [shape(rows, 2048, bf16), shape(rows, 2 * HEAD, f32), shape(rows, 3 * HEAD, bf16)],
            (gain, wk, wv, *powers, *hs), stay=(1, 2), scratch=held(wk, wv), flops=2 * rows * 2048 * 256,
        )

    x13, kv13, send13 = others((p1, p3), (h1u, h1l, h3u, h3l))
    got13 = rel(send13, "tr", 2, 1)
    x2, kv2, send2 = others((p2,), (h2u, h2l))
    got2 = rel(send2, "tr", 2, 1)
    q1, send_q = call(
        q_kernel, "q", [shape(3 * ROWS, QW, f32), shape(3 * ROWS, QW, bf16)], (x13, x2, wq),
        stay=(2,), scratch=held(wq), flops=6 * ROWS * 2048 * QW,
    )
    got_q = rel(send_q, "tr", 2, 1)
    got2, send_q = lax.optimization_barrier((got2, send_q))
    kv = call(
        rotary_kv_kernel, "rotary_kv", shape(BLOCK, 2 * HEAD, bf16), (kv0, got0, kv13, got13, kv2, got2, cosine, sine),
        flops=BLOCK * 256 * 8,
    )
    prev = lax.ppermute(kv, "ctx", [(i, i + 1) for i in range(lax.axis_size("ctx") - 1)])
    at, got = spread_far(kv, ctx)
    q = call(
        rotary_q_kernel, "rotary_q", shape(BLOCK, QW, bf16), (q0, got0, q1, got_q, cosine, sine),
        flops=BLOCK * 512 * 8,
    )
    got, q, prev = lax.optimization_barrier((got, q, prev))
    at = at + got[0] + got[1] + got[2]
    pre = (at, lax.ppermute(at, "ctx", [(2 * i, 2 * i + 1) for i in range(lax.axis_size("ctx") // 2)]))
    state = local(idx, lengths, q, kv, prev)
    parts = {}
    for r in (2, 1, 3, 0):
        parts[r] = finish(r, idx, lengths, state, q, pre, wo, f32 if r == 0 else bf16)
    total = parts[0]
    for r in (1, 3, 2):
        total = total + rel(parts[r], "tc", 4, -r).astype(f32)
    return (hidden.astype(f32) + total).astype(bf16)


def solution(mesh):
    in_specs = (
        P(("ctx", "tc"), "tr"),
        P("tr"),
        P(),
        P("tr", "tc"),
        P("tr", "tc"),
        P("tr", "tc"),
        P("tc", "tr"),
    )
    out_specs = P(("ctx", "tc"), "tr")
    return jax.shard_map(
        per_device, mesh=mesh, in_specs=in_specs, out_specs=out_specs, check_vma=False
    )
```

```python
import functools

import jax
import jax.numpy as jnp
from jax import lax
from jax.experimental import pallas as pl
from jax.experimental.pallas import tpu as pltpu
from jax.sharding import PartitionSpec as P

D = 4096
HEAD = 128
HALF = HEAD // 2
EPS = 1e-05
ROPE_BASE = 500000.0
MASKED = -1e30
ROWS = 128
HEADS = 4
QW = HEADS * HEAD
BLOCK = 512
SIDE = 1024
TAILED = HALF + 16
SCALE = HEAD ** (-0.5)
EXPONENT = SCALE * 1.4426950408889634

f32 = jnp.float32
bf16 = jnp.bfloat16


def spec(memory=pltpu.VMEM):
    return pl.BlockSpec(memory_space=memory)


def rel(x, axis, n, distance):
    return lax.ppermute(x, axis, [((i + distance) % n, i) for i in range(n)])


def call(kernel, name, out_shape, ins, smem=0, stay=(), scratch=(), vmem=24, flops=0, exps=0):
    many = isinstance(out_shape, list)
    ins = [pltpu.with_memory_space_constraint(x, pltpu.HBM) if n in stay else x for n, x in enumerate(ins)]
    where = [pltpu.SMEM] * smem + [pltpu.HBM if n in stay else pltpu.VMEM for n in range(smem, len(ins))]
    return pl.pallas_call(
        kernel,
        out_shape=out_shape,
        in_specs=[spec(w) for w in where],
        out_specs=[spec()] * len(out_shape) if many else spec(),
        scratch_shapes=list(scratch),
        compiler_params=pltpu.CompilerParams(vmem_limit_bytes=vmem << 20),
        cost_estimate=pl.CostEstimate(flops=flops, bytes_accessed=4 << 20, transcendentals=exps),
        name=name,
    )(*ins)


def square_column(n):
    return lax.broadcasted_iota(jnp.int32, (n, n), 0) == lax.broadcasted_iota(jnp.int32, (n, n), 1)


def fetch(sems, *pairs):
    copies = [pltpu.make_async_copy(src, dst, sems.at[n]) for n, (src, dst) in enumerate(pairs)]
    for copy in copies:
        copy.start()
    return copies


def squares_kernel(h_ref, upper_ref, lower_ref, out_ref, held, sems):
    fetch(sems, (h_ref, held))[0].wait()
    upper_ref[...] = held[:HALF, :]
    lower_ref[...] = held[HALF:, :]
    h = held[...].astype(f32)
    column = jnp.sum(h * h, axis=1, keepdims=True)
    row = jnp.sum(jnp.where(square_column(ROWS), column, 0.0), axis=0, keepdims=True)
    out_ref[...] = jnp.broadcast_to(row, (8, ROWS))


def normed(h, power, gain):
    return (h.astype(f32) * lax.rsqrt(power / D + EPS) * gain).astype(bf16)


def put_kv(x, wk_ref, wv_ref, keep_ref, send_ref):
    k = jnp.dot(x, wk_ref[...], preferred_element_type=f32)
    v = jnp.dot(x, wv_ref[...], preferred_element_type=f32)
    high = k.astype(bf16)
    keep_ref[:, :HEAD] = v
    keep_ref[:, HEAD:] = k
    send_ref[:, :HEAD] = v.astype(bf16)
    send_ref[:, HEAD : 2 * HEAD] = high
    send_ref[:, 2 * HEAD : 3 * HEAD] = (k - high.astype(f32)).astype(bf16)


def put_q(x, wq_ref, keep_ref, send_ref, at):
    q = jnp.dot(x, wq_ref[...], preferred_element_type=f32)
    keep_ref[...] = q
    send_ref[:, at : at + QW] = q.astype(bf16)


def tail_of(column):
    column = jnp.concatenate([column, jnp.zeros_like(column)], axis=0)
    row = jnp.sum(jnp.where(square_column(ROWS), column, 0.0), axis=0, keepdims=True)
    high = row.astype(bf16).astype(f32)
    middle = (row - high).astype(bf16).astype(f32)
    place = lax.broadcasted_iota(jnp.int32, (16, ROWS), 0)
    low = row - high - middle
    rows = jnp.where(place == 0, high, jnp.where(place == 1, middle, jnp.where(place == 2, low, 0.0)))
    return jnp.concatenate([rows, jnp.zeros((16, 2048 - ROWS), f32)], axis=1).astype(bf16)


def power_of(tail):
    row = jnp.sum(tail[:, :ROWS].astype(f32), axis=0, keepdims=True)
    return jnp.sum(jnp.where(square_column(ROWS), row, 0.0), axis=1, keepdims=True)[:HALF]


def prepare_kernel(mine_ref, theirs_ref, gain_ref, h_ref, upper_ref, lower_ref, h, sems):
    pending = fetch(sems, (h_ref, h))
    power = mine_ref[:1, :] + theirs_ref[:1, :]
    column = jnp.sum(jnp.where(square_column(ROWS), power, 0.0), axis=1, keepdims=True)
    upper_ref[HALF:, :] = tail_of(column[HALF:])
    lower_ref[HALF:, :] = tail_of(column[:HALF])
    pending[0].wait()
    x = normed(h[...], column, gain_ref[...])
    upper_ref[:HALF, :] = x[:HALF]
    lower_ref[:HALF, :] = x[HALF:]


def own_kernel(wq_ref, wk_ref, wv_ref, upper_ref, lower_ref, kv_ref, q_ref, send_ref, wq, wk, wv, sems):
    pending = fetch(sems, (wk_ref, wk), (wv_ref, wv), (wq_ref, wq))
    x = jnp.concatenate([upper_ref[:HALF, :], lower_ref[:HALF, :]], axis=0)
    pending[0].wait()
    pending[1].wait()
    put_kv(x, wk, wv, kv_ref, send_ref)
    pending[2].wait()
    put_q(x, wq, q_ref, send_ref, 3 * HEAD)


def near_kernel(wk_ref, wv_ref, gain_ref, h1u_ref, x1l_ref, x3u_ref, h3l_ref, x_ref, kv_ref, send_ref, wk, wv, sems):
    pending = fetch(sems, (wk_ref, wk), (wv_ref, wv))
    x_ref[:HALF, :] = normed(h1u_ref[...], power_of(x1l_ref[HALF:, :]), gain_ref[...])
    x_ref[HALF : 2 * HALF, :] = x1l_ref[:HALF, :]
    x_ref[2 * HALF : 3 * HALF, :] = x3u_ref[:HALF, :]
    x_ref[3 * HALF :, :] = normed(h3l_ref[...], power_of(x3u_ref[HALF:, :]), gain_ref[...])
    for copy in pending:
        copy.wait()
    put_kv(x_ref[...], wk, wv, kv_ref, send_ref)


def far_kernel(wk_ref, wv_ref, x2u_ref, x2l_ref, x_ref, kv_ref, send_ref, wk, wv, sems):
    pending = fetch(sems, (wk_ref, wk), (wv_ref, wv))
    x_ref[:HALF, :] = x2u_ref[:HALF, :]
    x_ref[HALF:, :] = x2l_ref[:HALF, :]
    for copy in pending:
        copy.wait()
    put_kv(x_ref[...], wk, wv, kv_ref, send_ref)


def q_kernel(xa_ref, xb_ref, wq_ref, keep_ref, send_ref, wq, sems):
    for copy in fetch(sems, (wq_ref, wq)):
        copy.wait()
    q = jnp.dot(jnp.concatenate([xa_ref[...], xb_ref[...]], axis=0), wq[...], preferred_element_type=f32)
    keep_ref[...] = q
    send_ref[...] = q.astype(bf16)


def rotated(u, cosine, sine):
    return (u * cosine + pltpu.roll(u, HALF, 1) * sine).astype(bf16)


def rotary_kv_kernel(keep0_ref, got0_ref, keepa_ref, gota_ref, keepb_ref, gotb_ref, cos_ref, sin_ref, kv_ref):
    for keep, got, s in (
        (keep0_ref, got0_ref, slice(0, ROWS)),
        (keepa_ref, gota_ref, slice(ROWS, 3 * ROWS)),
        (keepb_ref, gotb_ref, slice(3 * ROWS, BLOCK)),
    ):
        k = keep[:, HEAD:] + (
            got[:, HEAD : 2 * HEAD].astype(f32) + got[:, 2 * HEAD : 3 * HEAD].astype(f32)
        )
        kv_ref[s, :HEAD] = rotated(k, cos_ref[s, :], sin_ref[s, :])
        kv_ref[s, HEAD:] = (keep[:, :HEAD] + got[:, :HEAD].astype(f32)).astype(bf16)


def rotary_q_kernel(keep0_ref, got0_ref, keep_ref, got_ref, cos_ref, sin_ref, q_ref):
    for keep, got, s, at in (
        (keep0_ref, got0_ref, slice(0, ROWS), 3 * HEAD),
        (keep_ref, got_ref, slice(ROWS, BLOCK), 0),
    ):
        for h in range(HEADS):
            w = slice(h * HEAD, (h + 1) * HEAD)
            u = keep[:, w] + got[:, at + h * HEAD : at + (h + 1) * HEAD].astype(f32)
            q_ref[s, w] = rotated(u, cos_ref[s, :], sin_ref[s, :])


def chunk_of(ref, c):
    at = (0, 1, 3, 2)[c] * ROWS
    return ref[at : at + ROWS, :]


def stacked(q):
    return jnp.concatenate([q[:, h * HEAD : (h + 1) * HEAD] for h in range(HEADS)], axis=0)


def local_kernel(idx_ref, len_ref, q_ref, own_ref, prev_ref, acc_ref, max_ref, sum_ref, bias_ref):
    tc, ctx = idx_ref[0], idx_ref[1]
    lengths = len_ref[...].astype(f32)
    i = lax.broadcasted_iota(jnp.int32, (64, 64), 0)
    j = lax.broadcasted_iota(jnp.int32, (64, 64), 1)
    starts = jnp.sum(jnp.where(i < j, lengths, 0.0), axis=0, keepdims=True)
    prefix = jnp.sum(jnp.where(i[:, :1] < 1, lengths, 0.0), axis=0, keepdims=True).astype(jnp.int32)
    lane = lax.broadcasted_iota(jnp.int32, (ROWS, ROWS), 1)
    for r in range(4):
        a = (tc + r) % 4
        base = ctx * BLOCK + a * ROWS
        pos = base + lax.broadcasted_iota(jnp.int32, (ROWS, 64), 0)
        begun = jnp.where(starts <= pos.astype(f32), starts, 0.0)
        start = jnp.max(begun, axis=1, keepdims=True).astype(jnp.int32)
        t = base + lax.broadcasted_iota(jnp.int32, (ROWS, 1), 0)
        low = jnp.where(start >= prefix, start, jnp.int32(1 << 30))
        keys, values = [], []
        for n in range(5):
            c = (r + n) % 4
            if n == 0:
                chunk = chunk_of(prev_ref, c)
            elif n == 4:
                chunk = chunk_of(own_ref, c)
            else:
                chunk = jnp.where(a + n < 4, chunk_of(prev_ref, c), chunk_of(own_ref, c))
            keys.append(chunk[:, :HEAD])
            values.append(chunk[:, HEAD:])
            u = base + (n - 4) * ROWS + lane
            bias_ref[:, n * ROWS : (n + 1) * ROWS] = jnp.where((u >= low) & (u <= t), 0.0, MASKED)
        keys = jnp.concatenate(keys, axis=0)
        values = jnp.concatenate(values, axis=0)
        q = stacked(chunk_of(q_ref, r))
        s = lax.dot_general(q, keys, (((1,), (1,)), ((), ())), preferred_element_type=f32)
        s = (s.reshape(HEADS, ROWS, 5 * ROWS) + bias_ref[...][None]).reshape(BLOCK, 5 * ROWS)
        largest = jnp.max(s, axis=1, keepdims=True)
        p = jnp.exp2((s - largest) * EXPONENT)
        total = jnp.sum(p, axis=1, keepdims=True)
        acc_ref[r] = jnp.dot(p.astype(bf16), values, preferred_element_type=f32)
        max_ref[r] = jnp.broadcast_to(largest, (BLOCK, HEAD))
        sum_ref[r] = jnp.broadcast_to(total, (BLOCK, HEAD))


def local(idx, lengths, q, own, prev):
    shape = jax.ShapeDtypeStruct((4, BLOCK, HEAD), f32)
    return call(
        local_kernel, "local", [shape] * 3, (idx, lengths, q, own, prev), smem=1,
        scratch=[pltpu.VMEM((ROWS, 5 * ROWS), f32)], vmem=32,
        flops=4 * BLOCK * QW * 640, exps=4 * BLOCK * 640,
    )


def prefix_kernel(chunks, idx_ref, len_ref, acc_ref, max_ref, sum_ref, q_ref, pre_ref, other_ref, wo_ref, *refs):
    bias_ref, attended_ref = refs[-2:]
    tc, ctx = idx_ref[0], idx_ref[1]
    lengths = len_ref[...].astype(f32)
    i = lax.broadcasted_iota(jnp.int32, (64, 1), 0)
    prefix = jnp.sum(jnp.where(i < 1, lengths, 0.0), axis=0, keepdims=True).astype(jnp.int32)
    lane = lax.broadcasted_iota(jnp.int32, (ROWS, ROWS), 1)
    keys, values = [], []
    for c in range(4):
        chunk = chunk_of(pre_ref, c) + chunk_of(other_ref, c)
        keys.append(chunk[:, :HEAD])
        values.append(chunk[:, HEAD:])
    keys = jnp.concatenate(keys, axis=0)
    values = jnp.concatenate(values, axis=0)
    for n, r in enumerate(chunks):
        base = ctx * BLOCK + (tc + r) % 4 * ROWS
        high = jnp.minimum(prefix, base + 1 + lax.broadcasted_iota(jnp.int32, (ROWS, 1), 0))
        for c in range(4):
            u = ((tc + c) % 4) * ROWS + lane
            bias_ref[:, c * ROWS : (c + 1) * ROWS] = jnp.where(u < high, 0.0, MASKED)
        q = stacked(chunk_of(q_ref, r))
        s = lax.dot_general(q, keys, (((1,), (1,)), ((), ())), preferred_element_type=f32)
        s = (s.reshape(HEADS, ROWS, BLOCK) + bias_ref[...][None]).reshape(BLOCK, BLOCK)
        before = max_ref[r][:, :1]
        largest = jnp.maximum(jnp.max(s, axis=1, keepdims=True), before)
        p = jnp.exp2((s - largest) * EXPONENT)
        factor = jnp.exp2((before - largest) * EXPONENT)
        total = jnp.sum(p, axis=1, keepdims=True) + factor * sum_ref[r][:, :1]
        mixed = jnp.dot(p.astype(bf16), values, preferred_element_type=f32) + factor * acc_ref[r]
        mixed = (mixed / total).astype(bf16)
        for h in range(HEADS):
            attended_ref[n * ROWS : (n + 1) * ROWS, h * HEAD : (h + 1) * HEAD] = mixed[h * ROWS : (h + 1) * ROWS]
    for side, columns in ((0, slice(0, SIDE)), (1, slice(SIDE, 2 * SIDE))):
        out = jnp.dot(attended_ref[...], wo_ref[:, columns], preferred_element_type=f32)
        for n in range(len(chunks)):
            ref = refs[2 * n + side]
            ref[...] = out[n * ROWS : (n + 1) * ROWS].astype(ref.dtype)


def output_kernel(h_ref, *refs):
    for s, (own, one, two) in ((slice(0, SIDE), refs[:3]), (slice(SIDE, 2 * SIDE), refs[3:6])):
        total = own[...] + one[...].astype(f32) + two[...].astype(f32)
        refs[6][:, s] = (h_ref[:, s].astype(f32) + total).astype(bf16)


def finish(chunks, idx, lengths, state, q, pre, wo, kinds):
    n = len(chunks)
    return call(
        functools.partial(prefix_kernel, chunks), "prefix",
        [jax.ShapeDtypeStruct((ROWS, SIDE), kind) for kind in kinds],
        (idx, lengths, *state, q, *pre, wo), smem=1,
        scratch=[pltpu.VMEM((ROWS, BLOCK), f32), pltpu.VMEM((n * ROWS, QW), bf16)],
        flops=n * (4 * ROWS * QW * 512 + 2 * ROWS * QW * 2048), exps=4 * n * ROWS * 512,
    )


def first_kernel(idx_ref, x_ref, a_ref, b_ref, c_ref, out_ref):
    x = jnp.where(idx_ref[1] == 0, x_ref[...], jnp.zeros_like(x_ref))
    out_ref[...] = x + a_ref[...] + b_ref[...] + c_ref[...]


def second_kernel(x_ref, a_ref, b_ref, c_ref, out_ref):
    out_ref[...] = x_ref[...] + a_ref[...] + b_ref[...] + c_ref[...]


def spread_far(x, idx):
    got = [lax.ppermute(x, "ctx", [(0, 4 * z)]) for z in (2, 4, 6)]
    at = call(first_kernel, "first", jax.ShapeDtypeStruct(x.shape, x.dtype), (idx, x, *got), smem=1)
    return at, [lax.ppermute(at, "ctx", [(e, e + d) for e in (0, 8, 16, 24)]) for d in (4, 6, 2)]


def held(*arrays):
    return [pltpu.VMEM(a.shape, a.dtype) for a in arrays] + [pltpu.SemaphoreType.DMA((len(arrays),))]


def per_device(hidden, norm_gain, seg_lengths, wq, wk, wv, wo):
    tc = lax.axis_index("tc")
    ctx = lax.axis_index("ctx")
    idx = jnp.stack([tc, ctx]).astype(jnp.int32)
    def shape(rows, columns, dtype):
        return jax.ShapeDtypeStruct((rows, columns), dtype)

    upper, lower, mine = call(
        squares_kernel, "squares", [shape(HALF, 2048, bf16)] * 2 + [shape(8, ROWS, f32)], (hidden,), stay=(0,),
        scratch=held(hidden),
    )
    h1u = rel(upper, "tc", 4, 1)
    h3l = rel(lower, "tc", 4, 3)
    theirs = rel(mine, "tr", 2, 1)
    gain = norm_gain.reshape(1, -1)
    offset = (jnp.array([0, 1, 3, 2], jnp.int32) + tc) % 4 * ROWS
    positions = (ctx * BLOCK + offset[:, None] + jnp.arange(ROWS, dtype=jnp.int32)[None, :]).reshape(-1)
    frequency = ROPE_BASE ** (-(jnp.arange(HALF, dtype=f32) * 2.0 / HEAD))
    angles = positions.astype(f32)[:, None] * jnp.concatenate([frequency, frequency])[None, :]
    cosine = jnp.cos(angles)
    sine = jnp.sin(angles) * jnp.where(jnp.arange(HEAD) < HALF, -1.0, 1.0)[None, :]
    lengths = seg_lengths.reshape(-1, 1)

    xu, xl = call(
        prepare_kernel, "prepare", [shape(TAILED, 2048, bf16)] * 2, (mine, theirs, gain, hidden), stay=(3,),
        scratch=held(hidden), flops=ROWS * 2048 * 3,
    )
    x1l = rel(xl, "tc", 4, 1)
    x3u = rel(xu, "tc", 4, 3)
    kv0, q0, send0 = call(
        own_kernel, "own", [shape(ROWS, 2 * HEAD, f32), shape(ROWS, QW, f32), shape(ROWS, 7 * HEAD, bf16)],
        (wq, wk, wv, xu, xl), stay=(0, 1, 2), scratch=held(wq, wk, wv), flops=2 * ROWS * 2048 * 768,
    )
    x1l, x3u, send0 = lax.optimization_barrier((x1l, x3u, send0))
    x2l = rel(x1l, "tc", 4, 1)
    x2u = rel(x3u, "tc", 4, 3)
    got0 = rel(send0, "tr", 2, 1)
    x13, kv13, send13 = call(
        near_kernel, "near",
        [shape(2 * ROWS, 2048, bf16), shape(2 * ROWS, 2 * HEAD, f32), shape(2 * ROWS, 3 * HEAD, bf16)],
        (wk, wv, gain, h1u, x1l, x3u, h3l), stay=(0, 1), scratch=held(wk, wv), flops=4 * ROWS * 2048 * 256,
    )
    got13 = rel(send13, "tr", 2, 1)
    x2, kv2, send2 = call(
        far_kernel, "far",
        [shape(ROWS, 2048, bf16), shape(ROWS, 2 * HEAD, f32), shape(ROWS, 3 * HEAD, bf16)],
        (wk, wv, x2u, x2l), stay=(0, 1), scratch=held(wk, wv), flops=2 * ROWS * 2048 * 256,
    )
    got2 = rel(send2, "tr", 2, 1)
    q1, send_q = call(
        q_kernel, "q", [shape(3 * ROWS, QW, f32), shape(3 * ROWS, QW, bf16)], (x13, x2, wq),
        stay=(2,), scratch=held(wq), flops=6 * ROWS * 2048 * QW,
    )
    got_q = rel(send_q, "tr", 2, 1)
    got2, send_q = lax.optimization_barrier((got2, send_q))
    kv = call(
        rotary_kv_kernel, "rotary_kv", shape(BLOCK, 2 * HEAD, bf16), (kv0, got0, kv13, got13, kv2, got2, cosine, sine),
        flops=BLOCK * 256 * 8,
    )
    prev = lax.ppermute(kv, "ctx", [(i, i + 1) for i in range(lax.axis_size("ctx") - 1)])
    at, got = spread_far(kv, idx)
    q = call(
        rotary_q_kernel, "rotary_q", shape(BLOCK, QW, bf16), (q0, got0, q1, got_q, cosine, sine),
        flops=BLOCK * 512 * 8,
    )
    state = local(idx, lengths, q, kv, prev)
    got, state = lax.optimization_barrier((got, state))
    at = call(second_kernel, "second", shape(BLOCK, 2 * HEAD, bf16), (at, *got))
    pre = (at, lax.ppermute(at, "ctx", [(2 * i, 2 * i + 1) for i in range(lax.axis_size("ctx") // 2)]))
    args = (idx, lengths, state, q, pre, wo)
    left2, right2, left1, right1, left3, right3 = finish((2, 1, 3), *args, (bf16, bf16, f32, bf16, bf16, f32))
    left2, right2 = rel(left2, "tc", 4, -1), rel(right2, "tc", 4, 1)
    right1, left3 = rel(right1, "tc", 4, -1), rel(left3, "tc", 4, 1)
    left1 = rel((left1 + left2.astype(f32)).astype(bf16), "tc", 4, -1)
    right3 = rel((right3 + right2.astype(f32)).astype(bf16), "tc", 4, 1)
    left0, right0 = finish((0,), *args, (f32, f32))
    return call(
        output_kernel, "output", shape(ROWS, 2048, bf16),
        (hidden, left0, left1, left3, right0, right1, right3), flops=ROWS * 2048 * 3,
    )


def solution(mesh):
    in_specs = (
        P(("ctx", "tc"), "tr"),
        P("tr"),
        P(),
        P("tr", "tc"),
        P("tr", "tc"),
        P("tr", "tc"),
        P("tc", "tr"),
    )
    out_specs = P(("ctx", "tc"), "tr")
    return jax.shard_map(
        per_device, mesh=mesh, in_specs=in_specs, out_specs=out_specs, check_vma=False
    )
```

```python
import functools

import jax
import jax.numpy as jnp
from jax import lax
from jax.experimental import pallas as pl
from jax.experimental.pallas import tpu as pltpu
from jax.sharding import PartitionSpec as P

D = 4096
HEAD = 128
HALF = HEAD // 2
EPS = 1e-05
ROPE_BASE = 500000.0
MASKED = -1e30
ROWS = 128
HEADS = 4
QW = HEADS * HEAD
BLOCK = 512
SIDE = 1024
TAILED = HALF + 16
SCALE = HEAD ** (-0.5)
EXPONENT = SCALE * 1.4426950408889634

f32 = jnp.float32
bf16 = jnp.bfloat16


def spec(memory=pltpu.VMEM):
    return pl.BlockSpec(memory_space=memory)


def rel(x, axis, n, distance):
    return lax.ppermute(x, axis, [((i + distance) % n, i) for i in range(n)])


def call(kernel, name, out_shape, ins, smem=0, stay=(), scratch=(), vmem=24, flops=0, exps=0):
    many = isinstance(out_shape, list)
    ins = [pltpu.with_memory_space_constraint(x, pltpu.HBM) if n in stay else x for n, x in enumerate(ins)]
    where = [pltpu.SMEM] * smem + [pltpu.HBM if n in stay else pltpu.VMEM for n in range(smem, len(ins))]
    return pl.pallas_call(
        kernel,
        out_shape=out_shape,
        in_specs=[spec(w) for w in where],
        out_specs=[spec()] * len(out_shape) if many else spec(),
        scratch_shapes=list(scratch),
        compiler_params=pltpu.CompilerParams(vmem_limit_bytes=vmem << 20),
        cost_estimate=pl.CostEstimate(flops=flops, bytes_accessed=4 << 20, transcendentals=exps),
        name=name,
    )(*ins)


def square_column(n):
    return lax.broadcasted_iota(jnp.int32, (n, n), 0) == lax.broadcasted_iota(jnp.int32, (n, n), 1)


def fetch(sems, *pairs):
    copies = [pltpu.make_async_copy(src, dst, sems.at[n]) for n, (src, dst) in enumerate(pairs)]
    for copy in copies:
        copy.start()
    return copies


def squares_kernel(h_ref, upper_ref, lower_ref, out_ref, held, sems):
    fetch(sems, (h_ref, held))[0].wait()
    upper_ref[...] = held[:HALF, :]
    lower_ref[...] = held[HALF:, :]
    h = held[...].astype(f32)
    column = jnp.sum(h * h, axis=1, keepdims=True)
    row = jnp.sum(jnp.where(square_column(ROWS), column, 0.0), axis=0, keepdims=True)
    out_ref[...] = jnp.broadcast_to(row, (8, ROWS))


def normed(h, power, gain):
    return (h.astype(f32) * lax.rsqrt(power / D + EPS) * gain).astype(bf16)


def put_kv(x, wk_ref, wv_ref, keep_ref, send_ref):
    k = jnp.dot(x, wk_ref[...], preferred_element_type=f32)
    v = jnp.dot(x, wv_ref[...], preferred_element_type=f32)
    high = k.astype(bf16)
    keep_ref[:, :HEAD] = v
    keep_ref[:, HEAD:] = k
    send_ref[:, :HEAD] = v.astype(bf16)
    send_ref[:, HEAD : 2 * HEAD] = high
    send_ref[:, 2 * HEAD : 3 * HEAD] = (k - high.astype(f32)).astype(bf16)


def put_q(x, wq_ref, keep_ref, send_ref, at):
    q = jnp.dot(x, wq_ref[...], preferred_element_type=f32)
    keep_ref[...] = q
    send_ref[:, at : at + QW] = q.astype(bf16)


def tail_of(column):
    column = jnp.concatenate([column, jnp.zeros_like(column)], axis=0)
    row = jnp.sum(jnp.where(square_column(ROWS), column, 0.0), axis=0, keepdims=True)
    high = row.astype(bf16).astype(f32)
    middle = (row - high).astype(bf16).astype(f32)
    place = lax.broadcasted_iota(jnp.int32, (16, ROWS), 0)
    low = row - high - middle
    rows = jnp.where(place == 0, high, jnp.where(place == 1, middle, jnp.where(place == 2, low, 0.0)))
    return jnp.concatenate([rows, jnp.zeros((16, 2048 - ROWS), f32)], axis=1).astype(bf16)


def power_of(tail):
    row = jnp.sum(tail[:, :ROWS].astype(f32), axis=0, keepdims=True)
    return jnp.sum(jnp.where(square_column(ROWS), row, 0.0), axis=1, keepdims=True)[:HALF]


def prepare_kernel(mine_ref, theirs_ref, gain_ref, h_ref, upper_ref, lower_ref, power_ref, h, sems):
    pending = fetch(sems, (h_ref, h))
    power = mine_ref[:1, :] + theirs_ref[:1, :]
    power_ref[...] = jnp.broadcast_to(power, (8, ROWS))
    column = jnp.sum(jnp.where(square_column(ROWS), power, 0.0), axis=1, keepdims=True)
    upper_ref[HALF:, :] = tail_of(column[HALF:])
    lower_ref[HALF:, :] = tail_of(column[:HALF])
    pending[0].wait()
    x = normed(h[...], column, gain_ref[...])
    upper_ref[:HALF, :] = x[:HALF]
    lower_ref[:HALF, :] = x[HALF:]


def own_kernel(wq_ref, wk_ref, wv_ref, upper_ref, lower_ref, kv_ref, q_ref, send_ref, wq, wk, wv, sems):
    pending = fetch(sems, (wk_ref, wk), (wv_ref, wv), (wq_ref, wq))
    x = jnp.concatenate([upper_ref[:HALF, :], lower_ref[:HALF, :]], axis=0)
    pending[0].wait()
    pending[1].wait()
    put_kv(x, wk, wv, kv_ref, send_ref)
    pending[2].wait()
    put_q(x, wq, q_ref, send_ref, 3 * HEAD)


def near_kernel(wk_ref, wv_ref, gain_ref, h1u_ref, x1l_ref, x3u_ref, h3l_ref, x_ref, kv_ref, send_ref, wk, wv, sems):
    pending = fetch(sems, (wk_ref, wk), (wv_ref, wv))
    x_ref[:HALF, :] = normed(h1u_ref[...], power_of(x1l_ref[HALF:, :]), gain_ref[...])
    x_ref[HALF : 2 * HALF, :] = x1l_ref[:HALF, :]
    x_ref[2 * HALF : 3 * HALF, :] = x3u_ref[:HALF, :]
    x_ref[3 * HALF :, :] = normed(h3l_ref[...], power_of(x3u_ref[HALF:, :]), gain_ref[...])
    for copy in pending:
        copy.wait()
    put_kv(x_ref[...], wk, wv, kv_ref, send_ref)


def far_kernel(wk_ref, wv_ref, gain_ref, power_ref, h2u_ref, h2l_ref, x_ref, kv_ref, send_ref, wk, wv, sems):
    pending = fetch(sems, (wk_ref, wk), (wv_ref, wv))
    column = jnp.sum(jnp.where(square_column(ROWS), power_ref[:1, :], 0.0), axis=1, keepdims=True)
    h = jnp.concatenate([h2u_ref[...], h2l_ref[...]], axis=0)
    x_ref[...] = normed(h, column, gain_ref[...])
    for copy in pending:
        copy.wait()
    put_kv(x_ref[...], wk, wv, kv_ref, send_ref)


def q_kernel(xa_ref, xb_ref, wq_ref, keep_ref, send_ref):
    for x_ref, s in ((xa_ref, slice(0, 2 * ROWS)), (xb_ref, slice(2 * ROWS, 3 * ROWS))):
        q = jnp.dot(x_ref[...], wq_ref[...], preferred_element_type=f32)
        keep_ref[s, :] = q
        send_ref[s, :] = q.astype(bf16)


def rotated(u, cosine, sine):
    return (u * cosine + pltpu.roll(u, HALF, 1) * sine).astype(bf16)


def rotary_kv_kernel(keep0_ref, got0_ref, keepa_ref, gota_ref, keepb_ref, gotb_ref, cos_ref, sin_ref, kv_ref):
    for keep, got, s in (
        (keep0_ref, got0_ref, slice(0, ROWS)),
        (keepa_ref, gota_ref, slice(ROWS, 3 * ROWS)),
        (keepb_ref, gotb_ref, slice(3 * ROWS, BLOCK)),
    ):
        k = keep[:, HEAD:] + (
            got[:, HEAD : 2 * HEAD].astype(f32) + got[:, 2 * HEAD : 3 * HEAD].astype(f32)
        )
        kv_ref[s, :HEAD] = rotated(k, cos_ref[s, :], sin_ref[s, :])
        kv_ref[s, HEAD:] = (keep[:, :HEAD] + got[:, :HEAD].astype(f32)).astype(bf16)


def rotary_q_kernel(keep0_ref, got0_ref, keep_ref, got_ref, cos_ref, sin_ref, q_ref):
    for keep, got, s, at in (
        (keep0_ref, got0_ref, slice(0, ROWS), 3 * HEAD),
        (keep_ref, got_ref, slice(ROWS, BLOCK), 0),
    ):
        for h in range(HEADS):
            w = slice(h * HEAD, (h + 1) * HEAD)
            u = keep[:, w] + got[:, at + h * HEAD : at + (h + 1) * HEAD].astype(f32)
            q_ref[s, w] = rotated(u, cos_ref[s, :], sin_ref[s, :])


def chunk_of(ref, c):
    at = (0, 1, 3, 2)[c] * ROWS
    return ref[at : at + ROWS, :]


def stacked(q):
    return jnp.concatenate([q[:, h * HEAD : (h + 1) * HEAD] for h in range(HEADS)], axis=0)


def local_kernel(idx_ref, len_ref, q_ref, own_ref, prev_ref, acc_ref, max_ref, sum_ref, bias_ref):
    tc, ctx = idx_ref[0], idx_ref[1]
    lengths = len_ref[...].astype(f32)
    i = lax.broadcasted_iota(jnp.int32, (64, 64), 0)
    j = lax.broadcasted_iota(jnp.int32, (64, 64), 1)
    starts = jnp.sum(jnp.where(i < j, lengths, 0.0), axis=0, keepdims=True)
    prefix = jnp.sum(jnp.where(i[:, :1] < 1, lengths, 0.0), axis=0, keepdims=True).astype(jnp.int32)
    lane = lax.broadcasted_iota(jnp.int32, (ROWS, ROWS), 1)
    for r in range(4):
        a = (tc + r) % 4
        base = ctx * BLOCK + a * ROWS
        pos = base + lax.broadcasted_iota(jnp.int32, (ROWS, 64), 0)
        begun = jnp.where(starts <= pos.astype(f32), starts, 0.0)
        start = jnp.max(begun, axis=1, keepdims=True).astype(jnp.int32)
        t = base + lax.broadcasted_iota(jnp.int32, (ROWS, 1), 0)
        low = jnp.where(start >= prefix, start, jnp.int32(1 << 30))
        keys, values = [], []
        for n in range(5):
            c = (r + n) % 4
            if n == 0:
                chunk = chunk_of(prev_ref, c)
            elif n == 4:
                chunk = chunk_of(own_ref, c)
            else:
                chunk = jnp.where(a + n < 4, chunk_of(prev_ref, c), chunk_of(own_ref, c))
            keys.append(chunk[:, :HEAD])
            values.append(chunk[:, HEAD:])
            u = base + (n - 4) * ROWS + lane
            bias_ref[:, n * ROWS : (n + 1) * ROWS] = jnp.where((u >= low) & (u <= t), 0.0, MASKED)
        keys = jnp.concatenate(keys, axis=0)
        values = jnp.concatenate(values, axis=0)
        q = stacked(chunk_of(q_ref, r))
        s = lax.dot_general(q, keys, (((1,), (1,)), ((), ())), preferred_element_type=f32)
        s = (s.reshape(HEADS, ROWS, 5 * ROWS) + bias_ref[...][None]).reshape(BLOCK, 5 * ROWS)
        largest = jnp.max(s, axis=1, keepdims=True)
        p = jnp.exp2((s - largest) * EXPONENT)
        total = jnp.sum(p, axis=1, keepdims=True)
        acc_ref[r] = jnp.dot(p.astype(bf16), values, preferred_element_type=f32)
        max_ref[r] = jnp.broadcast_to(largest, (BLOCK, HEAD))
        sum_ref[r] = jnp.broadcast_to(total, (BLOCK, HEAD))


def local(idx, lengths, q, own, prev):
    shape = jax.ShapeDtypeStruct((4, BLOCK, HEAD), f32)
    return call(
        local_kernel, "local", [shape] * 3, (idx, lengths, q, own, prev), smem=1,
        scratch=[pltpu.VMEM((ROWS, 5 * ROWS), f32)], vmem=32,
        flops=4 * BLOCK * QW * 640, exps=4 * BLOCK * 640,
    )


def prefix_kernel(chunks, idx_ref, len_ref, acc_ref, max_ref, sum_ref, q_ref, pre_ref, other_ref, wo_ref, *refs):
    bias_ref, attended_ref = refs[-2:]
    tc, ctx = idx_ref[0], idx_ref[1]
    lengths = len_ref[...].astype(f32)
    i = lax.broadcasted_iota(jnp.int32, (64, 1), 0)
    prefix = jnp.sum(jnp.where(i < 1, lengths, 0.0), axis=0, keepdims=True).astype(jnp.int32)
    lane = lax.broadcasted_iota(jnp.int32, (ROWS, ROWS), 1)
    keys, values = [], []
    for c in range(4):
        chunk = chunk_of(pre_ref, c) + chunk_of(other_ref, c)
        keys.append(chunk[:, :HEAD])
        values.append(chunk[:, HEAD:])
    keys = jnp.concatenate(keys, axis=0)
    values = jnp.concatenate(values, axis=0)
    for n, r in enumerate(chunks):
        base = ctx * BLOCK + (tc + r) % 4 * ROWS
        high = jnp.minimum(prefix, base + 1 + lax.broadcasted_iota(jnp.int32, (ROWS, 1), 0))
        for c in range(4):
            u = ((tc + c) % 4) * ROWS + lane
            bias_ref[:, c * ROWS : (c + 1) * ROWS] = jnp.where(u < high, 0.0, MASKED)
        q = stacked(chunk_of(q_ref, r))
        s = lax.dot_general(q, keys, (((1,), (1,)), ((), ())), preferred_element_type=f32)
        s = (s.reshape(HEADS, ROWS, BLOCK) + bias_ref[...][None]).reshape(BLOCK, BLOCK)
        before = max_ref[r][:, :1]
        largest = jnp.maximum(jnp.max(s, axis=1, keepdims=True), before)
        p = jnp.exp2((s - largest) * EXPONENT)
        factor = jnp.exp2((before - largest) * EXPONENT)
        total = jnp.sum(p, axis=1, keepdims=True) + factor * sum_ref[r][:, :1]
        mixed = jnp.dot(p.astype(bf16), values, preferred_element_type=f32) + factor * acc_ref[r]
        mixed = (mixed / total).astype(bf16)
        for h in range(HEADS):
            attended_ref[n * ROWS : (n + 1) * ROWS, h * HEAD : (h + 1) * HEAD] = mixed[h * ROWS : (h + 1) * ROWS]
    for side, columns in ((0, slice(0, SIDE)), (1, slice(SIDE, 2 * SIDE))):
        out = jnp.dot(attended_ref[...], wo_ref[:, columns], preferred_element_type=f32)
        for n in range(len(chunks)):
            ref = refs[2 * n + side]
            ref[...] = out[n * ROWS : (n + 1) * ROWS].astype(ref.dtype)


def output_kernel(h_ref, *refs):
    for s, (own, one, two) in ((slice(0, SIDE), refs[:3]), (slice(SIDE, 2 * SIDE), refs[3:6])):
        total = own[...] + one[...].astype(f32) + two[...].astype(f32)
        refs[6][:, s] = (h_ref[:, s].astype(f32) + total).astype(bf16)


def finish(chunks, idx, lengths, state, q, pre, wo, kinds):
    n = len(chunks)
    return call(
        functools.partial(prefix_kernel, chunks), "prefix",
        [jax.ShapeDtypeStruct((ROWS, SIDE), kind) for kind in kinds],
        (idx, lengths, *state, q, *pre, wo), smem=1,
        scratch=[pltpu.VMEM((ROWS, BLOCK), f32), pltpu.VMEM((n * ROWS, QW), bf16)],
        flops=n * (4 * ROWS * QW * 512 + 2 * ROWS * QW * 2048), exps=4 * n * ROWS * 512,
    )


def first_kernel(idx_ref, x_ref, a_ref, b_ref, c_ref, out_ref):
    x = jnp.where(idx_ref[1] == 0, x_ref[...], jnp.zeros_like(x_ref))
    out_ref[...] = x + a_ref[...] + b_ref[...] + c_ref[...]


def second_kernel(x_ref, a_ref, b_ref, c_ref, out_ref):
    out_ref[...] = x_ref[...] + a_ref[...] + b_ref[...] + c_ref[...]


FIRST = ((1, 0), (7, 0), (4, 0))
SECOND = (
    {(1, 0): (2, 0), (7, 0): (6, 0), (4, 0): (3, 0), (0, 0): (5, 1)},
    {(1, 0): (2, 1), (7, 0): (6, 1), (4, 0): (5, 0), (0, 0): (3, 1)},
    {(1, 0): (1, 1), (7, 0): (7, 1), (4, 0): (4, 1), (0, 0): (0, 1)},
)


def even_index(chip):
    return 4 * chip[0] + 2 * chip[1]


def spread_far(x, idx):
    got = [lax.ppermute(x, "ctx", [(0, even_index(chip))]) for chip in FIRST]
    at = call(first_kernel, "first", jax.ShapeDtypeStruct(x.shape, x.dtype), (idx, x, *got), smem=1)
    return at, [
        lax.ppermute(at, "ctx", [(even_index(a), even_index(b)) for a, b in step.items()]) for step in SECOND
    ]


def held(*arrays):
    return [pltpu.VMEM(a.shape, a.dtype) for a in arrays] + [pltpu.SemaphoreType.DMA((len(arrays),))]


def per_device(hidden, norm_gain, seg_lengths, wq, wk, wv, wo):
    tc = lax.axis_index("tc")
    ctx = lax.axis_index("ctx")
    idx = jnp.stack([tc, ctx]).astype(jnp.int32)
    def shape(rows, columns, dtype):
        return jax.ShapeDtypeStruct((rows, columns), dtype)

    upper, lower, mine = call(
        squares_kernel, "squares", [shape(HALF, 2048, bf16)] * 2 + [shape(8, ROWS, f32)], (hidden,), stay=(0,),
        scratch=held(hidden),
    )
    h1u = rel(upper, "tc", 4, 1)
    h3l = rel(lower, "tc", 4, 3)
    theirs = rel(mine, "tr", 2, 1)
    gain = norm_gain.reshape(1, -1)
    offset = (jnp.array([0, 1, 3, 2], jnp.int32) + tc) % 4 * ROWS
    positions = (ctx * BLOCK + offset[:, None] + jnp.arange(ROWS, dtype=jnp.int32)[None, :]).reshape(-1)
    frequency = ROPE_BASE ** (-(jnp.arange(HALF, dtype=f32) * 2.0 / HEAD))
    angles = positions.astype(f32)[:, None] * jnp.concatenate([frequency, frequency])[None, :]
    cosine = jnp.cos(angles)
    sine = jnp.sin(angles) * jnp.where(jnp.arange(HEAD) < HALF, -1.0, 1.0)[None, :]
    lengths = seg_lengths.reshape(-1, 1)

    xu, xl, power = call(
        prepare_kernel, "prepare", [shape(TAILED, 2048, bf16)] * 2 + [shape(8, ROWS, f32)], (mine, theirs, gain, hidden), stay=(3,),
        scratch=held(hidden), flops=ROWS * 2048 * 3,
    )
    x1l = rel(xl, "tc", 4, 1)
    x3u = rel(xu, "tc", 4, 3)
    h2u = rel(h1u, "tc", 4, 1)
    h2l = rel(h3l, "tc", 4, 3)
    p2 = rel(power, "tc", 4, 2)
    own_u, _, _ = lax.optimization_barrier((xu, h1u, h3l))
    kv0, q0, send0 = call(
        own_kernel, "own", [shape(ROWS, 2 * HEAD, f32), shape(ROWS, QW, f32), shape(ROWS, 7 * HEAD, bf16)],
        (wq, wk, wv, own_u, xl), stay=(0, 1, 2), scratch=held(wq, wk, wv), flops=2 * ROWS * 2048 * 768,
    )
    got0 = rel(send0, "tr", 2, 1)
    x13, kv13, send13 = call(
        near_kernel, "near",
        [shape(2 * ROWS, 2048, bf16), shape(2 * ROWS, 2 * HEAD, f32), shape(2 * ROWS, 3 * HEAD, bf16)],
        (wk, wv, gain, h1u, x1l, x3u, h3l), stay=(0, 1), scratch=held(wk, wv), flops=4 * ROWS * 2048 * 256,
    )
    got13 = rel(send13, "tr", 2, 1)
    x2, kv2, send2 = call(
        far_kernel, "far",
        [shape(ROWS, 2048, bf16), shape(ROWS, 2 * HEAD, f32), shape(ROWS, 3 * HEAD, bf16)],
        (wk, wv, gain, p2, h2u, h2l), stay=(0, 1), scratch=held(wk, wv), flops=2 * ROWS * 2048 * 256,
    )
    got2 = rel(send2, "tr", 2, 1)
    q1, send_q = call(
        q_kernel, "q", [shape(3 * ROWS, QW, f32), shape(3 * ROWS, QW, bf16)], (x13, x2, wq), flops=6 * ROWS * 2048 * QW,
    )
    got_q = rel(send_q, "tr", 2, 1)
    got2, send_q = lax.optimization_barrier((got2, send_q))
    kv = call(
        rotary_kv_kernel, "rotary_kv", shape(BLOCK, 2 * HEAD, bf16), (kv0, got0, kv13, got13, kv2, got2, cosine, sine),
        flops=BLOCK * 256 * 8,
    )
    prev = lax.ppermute(kv, "ctx", [(i, i + 1) for i in range(lax.axis_size("ctx") - 1)])
    at, got = spread_far(kv, idx)
    q = call(
        rotary_q_kernel, "rotary_q", shape(BLOCK, QW, bf16), (q0, got0, q1, got_q, cosine, sine),
        flops=BLOCK * 512 * 8,
    )
    state = local(idx, lengths, q, kv, prev)
    got, state = lax.optimization_barrier((got, state))
    at = call(second_kernel, "second", shape(BLOCK, 2 * HEAD, bf16), (at, *got))
    pre = (at, lax.ppermute(at, "ctx", [(2 * i, 2 * i + 1) for i in range(lax.axis_size("ctx") // 2)]))
    args = (idx, lengths, state, q, pre, wo)
    left2, right2, left1, right1, left3, right3 = finish((2, 1, 3), *args, (bf16, bf16, f32, bf16, bf16, f32))
    left2, right2 = rel(left2, "tc", 4, -1), rel(right2, "tc", 4, 1)
    right1, left3 = rel(right1, "tc", 4, -1), rel(left3, "tc", 4, 1)
    left1 = rel((left1 + left2.astype(f32)).astype(bf16), "tc", 4, -1)
    right3 = rel((right3 + right2.astype(f32)).astype(bf16), "tc", 4, 1)
    left0, right0 = finish((0,), *args, (f32, f32))
    return call(
        output_kernel, "output", shape(ROWS, 2048, bf16),
        (hidden, left0, left1, left3, right0, right1, right3), flops=ROWS * 2048 * 3,
    )


def solution(mesh):
    in_specs = (
        P(("ctx", "tc"), "tr"),
        P("tr"),
        P(),
        P("tr", "tc"),
        P("tr", "tc"),
        P("tr", "tc"),
        P("tc", "tr"),
    )
    out_specs = P(("ctx", "tc"), "tr")
    return jax.shard_map(
        per_device, mesh=mesh, in_specs=in_specs, out_specs=out_specs, check_vma=False
    )
```

```python
import functools

import jax
import jax.numpy as jnp
from jax import lax
from jax.experimental import pallas as pl
from jax.experimental.pallas import tpu as pltpu
from jax.sharding import PartitionSpec as P

D = 4096
HEAD = 128
HALF = HEAD // 2
EPS = 1e-05
ROPE_BASE = 500000.0
MASKED = -1e30
ROWS = 128
HEADS = 4
QW = HEADS * HEAD
BLOCK = 512
SIDE = 1024
TAILED = HALF + 16
SCALE = HEAD ** (-0.5)
EXPONENT = SCALE * 1.4426950408889634

f32 = jnp.float32
bf16 = jnp.bfloat16


def spec(memory=pltpu.VMEM):
    return pl.BlockSpec(memory_space=memory)


def rel(x, axis, n, distance):
    return lax.ppermute(x, axis, [((i + distance) % n, i) for i in range(n)])


def call(kernel, name, out_shape, ins, smem=0, stay=(), scratch=(), vmem=24, flops=0, exps=0):
    many = isinstance(out_shape, list)
    ins = [pltpu.with_memory_space_constraint(x, pltpu.HBM) if n in stay else x for n, x in enumerate(ins)]
    where = [pltpu.SMEM] * smem + [pltpu.HBM if n in stay else pltpu.VMEM for n in range(smem, len(ins))]
    return pl.pallas_call(
        kernel,
        out_shape=out_shape,
        in_specs=[spec(w) for w in where],
        out_specs=[spec()] * len(out_shape) if many else spec(),
        scratch_shapes=list(scratch),
        compiler_params=pltpu.CompilerParams(vmem_limit_bytes=vmem << 20),
        cost_estimate=pl.CostEstimate(flops=flops, bytes_accessed=4 << 20, transcendentals=exps),
        name=name,
    )(*ins)


def square_column(n):
    return lax.broadcasted_iota(jnp.int32, (n, n), 0) == lax.broadcasted_iota(jnp.int32, (n, n), 1)


def fetch(sems, *pairs):
    copies = [pltpu.make_async_copy(src, dst, sems.at[n]) for n, (src, dst) in enumerate(pairs)]
    for copy in copies:
        copy.start()
    return copies


def squares_kernel(h_ref, upper_ref, lower_ref, out_ref, held, sems):
    fetch(sems, (h_ref, held))[0].wait()
    upper_ref[...] = held[:HALF, :]
    lower_ref[...] = held[HALF:, :]
    h = held[...].astype(f32)
    column = jnp.sum(h * h, axis=1, keepdims=True)
    row = jnp.sum(jnp.where(square_column(ROWS), column, 0.0), axis=0, keepdims=True)
    out_ref[...] = jnp.broadcast_to(row, (8, ROWS))


def normed(h, power, gain):
    return (h.astype(f32) * lax.rsqrt(power / D + EPS) * gain).astype(bf16)


def put_kv(x, wk_ref, wv_ref, keep_ref, send_ref):
    k = jnp.dot(x, wk_ref[...], preferred_element_type=f32)
    v = jnp.dot(x, wv_ref[...], preferred_element_type=f32)
    high = k.astype(bf16)
    keep_ref[:, :HEAD] = v
    keep_ref[:, HEAD:] = k
    send_ref[:, :HEAD] = v.astype(bf16)
    send_ref[:, HEAD : 2 * HEAD] = high
    send_ref[:, 2 * HEAD : 3 * HEAD] = (k - high.astype(f32)).astype(bf16)


def put_q(x, wq_ref, keep_ref, send_ref, at):
    q = jnp.dot(x, wq_ref[...], preferred_element_type=f32)
    keep_ref[...] = q
    send_ref[:, at : at + QW] = q.astype(bf16)


def tail_of(column):
    column = jnp.concatenate([column, jnp.zeros_like(column)], axis=0)
    row = jnp.sum(jnp.where(square_column(ROWS), column, 0.0), axis=0, keepdims=True)
    high = row.astype(bf16).astype(f32)
    middle = (row - high).astype(bf16).astype(f32)
    place = lax.broadcasted_iota(jnp.int32, (16, ROWS), 0)
    low = row - high - middle
    rows = jnp.where(place == 0, high, jnp.where(place == 1, middle, jnp.where(place == 2, low, 0.0)))
    return jnp.concatenate([rows, jnp.zeros((16, 2048 - ROWS), f32)], axis=1).astype(bf16)


def power_of(tail):
    row = jnp.sum(tail[:, :ROWS].astype(f32), axis=0, keepdims=True)
    return jnp.sum(jnp.where(square_column(ROWS), row, 0.0), axis=1, keepdims=True)[:HALF]


def prepare_kernel(mine_ref, theirs_ref, gain_ref, h_ref, upper_ref, lower_ref, power_ref, h, sems):
    pending = fetch(sems, (h_ref, h))
    power = mine_ref[:1, :] + theirs_ref[:1, :]
    power_ref[...] = jnp.broadcast_to(power, (8, ROWS))
    column = jnp.sum(jnp.where(square_column(ROWS), power, 0.0), axis=1, keepdims=True)
    upper_ref[HALF:, :] = tail_of(column[HALF:])
    lower_ref[HALF:, :] = tail_of(column[:HALF])
    pending[0].wait()
    x = normed(h[...], column, gain_ref[...])
    upper_ref[:HALF, :] = x[:HALF]
    lower_ref[:HALF, :] = x[HALF:]


def own_kernel(wq_ref, wk_ref, wv_ref, upper_ref, lower_ref, kv_ref, q_ref, send_ref, wq, wk, wv, sems):
    pending = fetch(sems, (wk_ref, wk), (wv_ref, wv), (wq_ref, wq))
    x = jnp.concatenate([upper_ref[:HALF, :], lower_ref[:HALF, :]], axis=0)
    pending[0].wait()
    pending[1].wait()
    put_kv(x, wk, wv, kv_ref, send_ref)
    pending[2].wait()
    put_q(x, wq, q_ref, send_ref, 3 * HEAD)


def near_kernel(wk_ref, wv_ref, gain_ref, h1u_ref, x1l_ref, x3u_ref, h3l_ref, x_ref, kv_ref, send_ref, wk, wv, sems):
    pending = fetch(sems, (wk_ref, wk), (wv_ref, wv))
    x_ref[:HALF, :] = normed(h1u_ref[...], power_of(x1l_ref[HALF:, :]), gain_ref[...])
    x_ref[HALF : 2 * HALF, :] = x1l_ref[:HALF, :]
    x_ref[2 * HALF : 3 * HALF, :] = x3u_ref[:HALF, :]
    x_ref[3 * HALF :, :] = normed(h3l_ref[...], power_of(x3u_ref[HALF:, :]), gain_ref[...])
    for copy in pending:
        copy.wait()
    put_kv(x_ref[...], wk, wv, kv_ref, send_ref)


def far_kernel(wk_ref, wv_ref, gain_ref, power_ref, h2u_ref, h2l_ref, x_ref, kv_ref, send_ref, wk, wv, sems):
    pending = fetch(sems, (wk_ref, wk), (wv_ref, wv))
    column = jnp.sum(jnp.where(square_column(ROWS), power_ref[:1, :], 0.0), axis=1, keepdims=True)
    h = jnp.concatenate([h2u_ref[...], h2l_ref[...]], axis=0)
    x_ref[...] = normed(h, column, gain_ref[...])
    for copy in pending:
        copy.wait()
    put_kv(x_ref[...], wk, wv, kv_ref, send_ref)


def q_kernel(xa_ref, xb_ref, wq_ref, keep_ref, send_ref):
    for x_ref, s in ((xa_ref, slice(0, 2 * ROWS)), (xb_ref, slice(2 * ROWS, 3 * ROWS))):
        q = jnp.dot(x_ref[...], wq_ref[...], preferred_element_type=f32)
        keep_ref[s, :] = q
        send_ref[s, :] = q.astype(bf16)


def rotated(u, cosine, sine):
    return (u * cosine + pltpu.roll(u, HALF, 1) * sine).astype(bf16)


def rotary_kv_kernel(keep0_ref, got0_ref, keepa_ref, gota_ref, keepb_ref, gotb_ref, cos_ref, sin_ref, kv_ref):
    for keep, got, s in (
        (keep0_ref, got0_ref, slice(0, ROWS)),
        (keepa_ref, gota_ref, slice(ROWS, 3 * ROWS)),
        (keepb_ref, gotb_ref, slice(3 * ROWS, BLOCK)),
    ):
        k = keep[:, HEAD:] + (
            got[:, HEAD : 2 * HEAD].astype(f32) + got[:, 2 * HEAD : 3 * HEAD].astype(f32)
        )
        kv_ref[s, :HEAD] = rotated(k, cos_ref[s, :], sin_ref[s, :])
        kv_ref[s, HEAD:] = (keep[:, :HEAD] + got[:, :HEAD].astype(f32)).astype(bf16)


def rotary_q_kernel(keep0_ref, got0_ref, keep_ref, got_ref, cos_ref, sin_ref, q_ref):
    for keep, got, s, at in (
        (keep0_ref, got0_ref, slice(0, ROWS), 3 * HEAD),
        (keep_ref, got_ref, slice(ROWS, BLOCK), 0),
    ):
        for h in range(HEADS):
            w = slice(h * HEAD, (h + 1) * HEAD)
            u = keep[:, w] + got[:, at + h * HEAD : at + (h + 1) * HEAD].astype(f32)
            q_ref[s, w] = rotated(u, cos_ref[s, :], sin_ref[s, :])


def chunk_of(ref, c):
    at = (0, 1, 3, 2)[c] * ROWS
    return ref[at : at + ROWS, :]


def stacked(q):
    return jnp.concatenate([q[:, h * HEAD : (h + 1) * HEAD] for h in range(HEADS)], axis=0)


def local_kernel(idx_ref, len_ref, q_ref, own_ref, prev_ref, acc_ref, max_ref, sum_ref, bias_ref):
    tc, ctx = idx_ref[0], idx_ref[1]
    lengths = len_ref[...].astype(f32)
    i = lax.broadcasted_iota(jnp.int32, (64, 64), 0)
    j = lax.broadcasted_iota(jnp.int32, (64, 64), 1)
    starts = jnp.sum(jnp.where(i < j, lengths, 0.0), axis=0, keepdims=True)
    prefix = jnp.sum(jnp.where(i[:, :1] < 1, lengths, 0.0), axis=0, keepdims=True).astype(jnp.int32)
    lane = lax.broadcasted_iota(jnp.int32, (ROWS, ROWS), 1)
    for r in range(4):
        a = (tc + r) % 4
        base = ctx * BLOCK + a * ROWS
        pos = base + lax.broadcasted_iota(jnp.int32, (ROWS, 64), 0)
        begun = jnp.where(starts <= pos.astype(f32), starts, 0.0)
        start = jnp.max(begun, axis=1, keepdims=True).astype(jnp.int32)
        t = base + lax.broadcasted_iota(jnp.int32, (ROWS, 1), 0)
        low = jnp.where(start >= prefix, start, jnp.int32(1 << 30))
        keys, values = [], []
        for n in range(5):
            c = (r + n) % 4
            if n == 0:
                chunk = chunk_of(prev_ref, c)
            elif n == 4:
                chunk = chunk_of(own_ref, c)
            else:
                chunk = jnp.where(a + n < 4, chunk_of(prev_ref, c), chunk_of(own_ref, c))
            keys.append(chunk[:, :HEAD])
            values.append(chunk[:, HEAD:])
            u = base + (n - 4) * ROWS + lane
            bias_ref[:, n * ROWS : (n + 1) * ROWS] = jnp.where((u >= low) & (u <= t), 0.0, MASKED)
        keys = jnp.concatenate(keys, axis=0)
        values = jnp.concatenate(values, axis=0)
        q = stacked(chunk_of(q_ref, r))
        s = lax.dot_general(q, keys, (((1,), (1,)), ((), ())), preferred_element_type=f32)
        s = (s.reshape(HEADS, ROWS, 5 * ROWS) + bias_ref[...][None]).reshape(BLOCK, 5 * ROWS)
        largest = jnp.max(s, axis=1, keepdims=True)
        p = jnp.exp2((s - largest) * EXPONENT)
        total = jnp.sum(p, axis=1, keepdims=True)
        acc_ref[r] = jnp.dot(p.astype(bf16), values, preferred_element_type=f32)
        max_ref[r] = jnp.broadcast_to(largest, (BLOCK, HEAD))
        sum_ref[r] = jnp.broadcast_to(total, (BLOCK, HEAD))


def local(idx, lengths, q, own, prev):
    shape = jax.ShapeDtypeStruct((4, BLOCK, HEAD), f32)
    return call(
        local_kernel, "local", [shape] * 3, (idx, lengths, q, own, prev), smem=1,
        scratch=[pltpu.VMEM((ROWS, 5 * ROWS), f32)], vmem=32,
        flops=4 * BLOCK * QW * 640, exps=4 * BLOCK * 640,
    )


def prefix_kernel(chunks, idx_ref, len_ref, acc_ref, max_ref, sum_ref, q_ref, pre_ref, other_ref, wo_ref, *refs):
    bias_ref, attended_ref = refs[-2:]
    tc, ctx = idx_ref[0], idx_ref[1]
    lengths = len_ref[...].astype(f32)
    i = lax.broadcasted_iota(jnp.int32, (64, 1), 0)
    prefix = jnp.sum(jnp.where(i < 1, lengths, 0.0), axis=0, keepdims=True).astype(jnp.int32)
    lane = lax.broadcasted_iota(jnp.int32, (ROWS, ROWS), 1)
    keys, values = [], []
    for c in range(4):
        chunk = chunk_of(pre_ref, c) + chunk_of(other_ref, c)
        keys.append(chunk[:, :HEAD])
        values.append(chunk[:, HEAD:])
    keys = jnp.concatenate(keys, axis=0)
    values = jnp.concatenate(values, axis=0)
    for n, r in enumerate(chunks):
        base = ctx * BLOCK + (tc + r) % 4 * ROWS
        high = jnp.minimum(prefix, base + 1 + lax.broadcasted_iota(jnp.int32, (ROWS, 1), 0))
        for c in range(4):
            u = ((tc + c) % 4) * ROWS + lane
            bias_ref[:, c * ROWS : (c + 1) * ROWS] = jnp.where(u < high, 0.0, MASKED)
        q = stacked(chunk_of(q_ref, r))
        s = lax.dot_general(q, keys, (((1,), (1,)), ((), ())), preferred_element_type=f32)
        s = (s.reshape(HEADS, ROWS, BLOCK) + bias_ref[...][None]).reshape(BLOCK, BLOCK)
        before = max_ref[r][:, :1]
        largest = jnp.maximum(jnp.max(s, axis=1, keepdims=True), before)
        p = jnp.exp2((s - largest) * EXPONENT)
        factor = jnp.exp2((before - largest) * EXPONENT)
        total = jnp.sum(p, axis=1, keepdims=True) + factor * sum_ref[r][:, :1]
        mixed = jnp.dot(p.astype(bf16), values, preferred_element_type=f32) + factor * acc_ref[r]
        mixed = (mixed / total).astype(bf16)
        for h in range(HEADS):
            attended_ref[n * ROWS : (n + 1) * ROWS, h * HEAD : (h + 1) * HEAD] = mixed[h * ROWS : (h + 1) * ROWS]
    for side, columns in ((0, slice(0, SIDE)), (1, slice(SIDE, 2 * SIDE))):
        out = jnp.dot(attended_ref[...], wo_ref[:, columns], preferred_element_type=f32)
        for n in range(len(chunks)):
            ref = refs[2 * n + side]
            ref[...] = out[n * ROWS : (n + 1) * ROWS].astype(ref.dtype)


def output_kernel(h_ref, *refs):
    for s, (own, one, two) in ((slice(0, SIDE), refs[:3]), (slice(SIDE, 2 * SIDE), refs[3:6])):
        total = own[...] + one[...].astype(f32) + two[...].astype(f32)
        refs[6][:, s] = (h_ref[:, s].astype(f32) + total).astype(bf16)


def finish(chunks, idx, lengths, state, q, pre, wo, kinds):
    n = len(chunks)
    return call(
        functools.partial(prefix_kernel, chunks), "prefix",
        [jax.ShapeDtypeStruct((ROWS, SIDE), kind) for kind in kinds],
        (idx, lengths, *state, q, *pre, wo), smem=1,
        scratch=[pltpu.VMEM((ROWS, BLOCK), f32), pltpu.VMEM((n * ROWS, QW), bf16)],
        flops=n * (4 * ROWS * QW * 512 + 2 * ROWS * QW * 2048), exps=4 * n * ROWS * 512,
    )


def first_kernel(idx_ref, x_ref, a_ref, b_ref, c_ref, out_ref):
    x = jnp.where(idx_ref[1] == 0, x_ref[...], jnp.zeros_like(x_ref))
    out_ref[...] = x + a_ref[...] + b_ref[...] + c_ref[...]


def second_kernel(x_ref, a_ref, b_ref, c_ref, out_ref):
    out_ref[...] = x_ref[...] + a_ref[...] + b_ref[...] + c_ref[...]


FIRST = ((1, 0), (7, 0), (4, 0))
SECOND = (
    {(1, 0): (2, 0), (7, 0): (6, 0), (4, 0): (3, 0), (0, 0): (5, 1)},
    {(1, 0): (2, 1), (7, 0): (6, 1), (4, 0): (5, 0), (0, 0): (3, 1)},
    {(1, 0): (1, 1), (7, 0): (7, 1), (4, 0): (4, 1), (0, 0): (0, 1)},
)


def even_index(chip):
    return 4 * chip[0] + 2 * chip[1]


def spread_far(x, idx):
    got = [lax.ppermute(x, "ctx", [(0, even_index(chip))]) for chip in FIRST]
    at = call(first_kernel, "first", jax.ShapeDtypeStruct(x.shape, x.dtype), (idx, x, *got), smem=1)
    return at, [
        lax.ppermute(at, "ctx", [(even_index(a), even_index(b)) for a, b in step.items()]) for step in SECOND
    ]


def held(*arrays):
    return [pltpu.VMEM(a.shape, a.dtype) for a in arrays] + [pltpu.SemaphoreType.DMA((len(arrays),))]


def per_device(hidden, norm_gain, seg_lengths, wq, wk, wv, wo):
    tc = lax.axis_index("tc")
    ctx = lax.axis_index("ctx")
    idx = jnp.stack([tc, ctx]).astype(jnp.int32)
    def shape(rows, columns, dtype):
        return jax.ShapeDtypeStruct((rows, columns), dtype)

    upper, lower, mine = call(
        squares_kernel, "squares", [shape(HALF, 2048, bf16)] * 2 + [shape(8, ROWS, f32)], (hidden,), stay=(0,),
        scratch=held(hidden),
    )
    h1u = rel(upper, "tc", 4, 1)
    h3l = rel(lower, "tc", 4, 3)
    theirs = rel(mine, "tr", 2, 1)
    gain = norm_gain.reshape(1, -1)
    offset = (jnp.array([0, 1, 3, 2], jnp.int32) + tc) % 4 * ROWS
    positions = (ctx * BLOCK + offset[:, None] + jnp.arange(ROWS, dtype=jnp.int32)[None, :]).reshape(-1)
    frequency = ROPE_BASE ** (-(jnp.arange(HALF, dtype=f32) * 2.0 / HEAD))
    angles = positions.astype(f32)[:, None] * jnp.concatenate([frequency, frequency])[None, :]
    cosine = jnp.cos(angles)
    sine = jnp.sin(angles) * jnp.where(jnp.arange(HEAD) < HALF, -1.0, 1.0)[None, :]
    lengths = seg_lengths.reshape(-1, 1)

    xu, xl, power = call(
        prepare_kernel, "prepare", [shape(TAILED, 2048, bf16)] * 2 + [shape(8, ROWS, f32)], (mine, theirs, gain, hidden), stay=(3,),
        scratch=held(hidden), flops=ROWS * 2048 * 3,
    )
    x1l = rel(xl, "tc", 4, 1)
    x3u = rel(xu, "tc", 4, 3)
    h2u = rel(h1u, "tc", 4, 1)
    h2l = rel(h3l, "tc", 4, 3)
    p2 = rel(power, "tc", 4, 2)
    own_u, _, _ = lax.optimization_barrier((xu, h1u, h3l))
    kv0, q0, send0 = call(
        own_kernel, "own", [shape(ROWS, 2 * HEAD, f32), shape(ROWS, QW, f32), shape(ROWS, 7 * HEAD, bf16)],
        (wq, wk, wv, own_u, xl), stay=(0, 1, 2), scratch=held(wq, wk, wv), flops=2 * ROWS * 2048 * 768,
    )
    got0 = rel(send0, "tr", 2, 1)
    x13, kv13, send13 = call(
        near_kernel, "near",
        [shape(2 * ROWS, 2048, bf16), shape(2 * ROWS, 2 * HEAD, f32), shape(2 * ROWS, 3 * HEAD, bf16)],
        (wk, wv, gain, h1u, x1l, x3u, h3l), stay=(0, 1), scratch=held(wk, wv), flops=4 * ROWS * 2048 * 256,
    )
    got13 = rel(send13, "tr", 2, 1)
    x2, kv2, send2 = call(
        far_kernel, "far",
        [shape(ROWS, 2048, bf16), shape(ROWS, 2 * HEAD, f32), shape(ROWS, 3 * HEAD, bf16)],
        (wk, wv, gain, p2, h2u, h2l), stay=(0, 1), scratch=held(wk, wv), flops=2 * ROWS * 2048 * 256,
    )
    got2 = rel(send2, "tr", 2, 1)
    q1, send_q = call(
        q_kernel, "q", [shape(3 * ROWS, QW, f32), shape(3 * ROWS, QW, bf16)], (x13, x2, wq), flops=6 * ROWS * 2048 * QW,
    )
    got_q = rel(send_q, "tr", 2, 1)
    got2, send_q = lax.optimization_barrier((got2, send_q))
    kv = call(
        rotary_kv_kernel, "rotary_kv", shape(BLOCK, 2 * HEAD, bf16), (kv0, got0, kv13, got13, kv2, got2, cosine, sine),
        flops=BLOCK * 256 * 8,
    )
    prev = lax.ppermute(kv, "ctx", [(i, i + 1) for i in range(lax.axis_size("ctx") - 1)])
    at, got = spread_far(kv, idx)
    q = call(
        rotary_q_kernel, "rotary_q", shape(BLOCK, QW, bf16), (q0, got0, q1, got_q, cosine, sine),
        flops=BLOCK * 512 * 8,
    )
    state = local(idx, lengths, q, kv, prev)
    got, state = lax.optimization_barrier((got, state))
    at = call(second_kernel, "second", shape(BLOCK, 2 * HEAD, bf16), (at, *got))
    pre = (at, lax.ppermute(at, "ctx", [(2 * i, 2 * i + 1) for i in range(lax.axis_size("ctx") // 2)]))
    args = (idx, lengths, state, q, pre, wo)
    left2, right2 = finish((2,), *args, (bf16, bf16))
    left2, right2 = rel(left2, "tc", 4, -1), rel(right2, "tc", 4, 1)
    left1, right1, left3, right3 = finish((1, 3), *args, (f32, bf16, bf16, f32))
    right1, left3 = rel(right1, "tc", 4, -1), rel(left3, "tc", 4, 1)
    left1 = rel((left1 + left2.astype(f32)).astype(bf16), "tc", 4, -1)
    right3 = rel((right3 + right2.astype(f32)).astype(bf16), "tc", 4, 1)
    left0, right0 = finish((0,), *args, (f32, f32))
    return call(
        output_kernel, "output", shape(ROWS, 2048, bf16),
        (hidden, left0, left1, left3, right0, right1, right3), flops=ROWS * 2048 * 3,
    )


def solution(mesh):
    in_specs = (
        P(("ctx", "tc"), "tr"),
        P("tr"),
        P(),
        P("tr", "tc"),
        P("tr", "tc"),
        P("tr", "tc"),
        P("tc", "tr"),
    )
    out_specs = P(("ctx", "tc"), "tr")
    return jax.shard_map(
        per_device, mesh=mesh, in_specs=in_specs, out_specs=out_specs, check_vma=False
    )
```

```python
import functools

import jax
import jax.numpy as jnp
from jax import lax
from jax.experimental import pallas as pl
from jax.experimental.pallas import tpu as pltpu
from jax.sharding import PartitionSpec as P

D = 4096
HEAD = 128
HALF = HEAD // 2
EPS = 1e-05
ROPE_BASE = 500000.0
MASKED = -1e30
ROWS = 128
HEADS = 4
QW = HEADS * HEAD
BLOCK = 512
SIDE = 1024
TAILED = HALF + 16
SCALE = HEAD ** (-0.5)
EXPONENT = SCALE * 1.4426950408889634

f32 = jnp.float32
bf16 = jnp.bfloat16


def spec(memory=pltpu.VMEM):
    return pl.BlockSpec(memory_space=memory)


def rel(x, axis, n, distance):
    return lax.ppermute(x, axis, [((i + distance) % n, i) for i in range(n)])


def call(kernel, name, out_shape, ins, smem=0, stay=(), scratch=(), vmem=24, flops=0, exps=0):
    many = isinstance(out_shape, list)
    ins = [pltpu.with_memory_space_constraint(x, pltpu.HBM) if n in stay else x for n, x in enumerate(ins)]
    where = [pltpu.SMEM] * smem + [pltpu.HBM if n in stay else pltpu.VMEM for n in range(smem, len(ins))]
    return pl.pallas_call(
        kernel,
        out_shape=out_shape,
        in_specs=[spec(w) for w in where],
        out_specs=[spec()] * len(out_shape) if many else spec(),
        scratch_shapes=list(scratch),
        compiler_params=pltpu.CompilerParams(vmem_limit_bytes=vmem << 20),
        cost_estimate=pl.CostEstimate(flops=flops, bytes_accessed=4 << 20, transcendentals=exps),
        name=name,
    )(*ins)


def square_column(n):
    return lax.broadcasted_iota(jnp.int32, (n, n), 0) == lax.broadcasted_iota(jnp.int32, (n, n), 1)


def fetch(sems, *pairs):
    copies = [pltpu.make_async_copy(src, dst, sems.at[n]) for n, (src, dst) in enumerate(pairs)]
    for copy in copies:
        copy.start()
    return copies


def squares_kernel(h_ref, upper_ref, lower_ref, out_ref, held, sems):
    fetch(sems, (h_ref, held))[0].wait()
    upper_ref[...] = held[:HALF, :]
    lower_ref[...] = held[HALF:, :]
    h = held[...].astype(f32)
    column = jnp.sum(h * h, axis=1, keepdims=True)
    row = jnp.sum(jnp.where(square_column(ROWS), column, 0.0), axis=0, keepdims=True)
    out_ref[...] = jnp.broadcast_to(row, (8, ROWS))


def normed(h, power, gain):
    return (h.astype(f32) * lax.rsqrt(power / D + EPS) * gain).astype(bf16)


def put_kv(x, wk_ref, wv_ref, keep_ref, send_ref, pending):
    pending[0].wait()
    k = jnp.dot(x, wk_ref[...], preferred_element_type=f32)
    pending[1].wait()
    v = jnp.dot(x, wv_ref[...], preferred_element_type=f32)
    high = k.astype(bf16)
    keep_ref[:, :HEAD] = v
    keep_ref[:, HEAD:] = k
    send_ref[:, :HEAD] = v.astype(bf16)
    send_ref[:, HEAD : 2 * HEAD] = high
    send_ref[:, 2 * HEAD : 3 * HEAD] = (k - high.astype(f32)).astype(bf16)


def put_q(x, wq_ref, keep_ref, send_ref, at):
    q = jnp.dot(x, wq_ref[...], preferred_element_type=f32)
    keep_ref[...] = q
    send_ref[:, at : at + QW] = q.astype(bf16)


def tail_of(column):
    column = jnp.concatenate([column, jnp.zeros_like(column)], axis=0)
    row = jnp.sum(jnp.where(square_column(ROWS), column, 0.0), axis=0, keepdims=True)
    high = row.astype(bf16).astype(f32)
    middle = (row - high).astype(bf16).astype(f32)
    place = lax.broadcasted_iota(jnp.int32, (16, ROWS), 0)
    low = row - high - middle
    rows = jnp.where(place == 0, high, jnp.where(place == 1, middle, jnp.where(place == 2, low, 0.0)))
    return jnp.concatenate([rows, jnp.zeros((16, 2048 - ROWS), f32)], axis=1).astype(bf16)


def power_of(tail):
    row = jnp.sum(tail[:, :ROWS].astype(f32), axis=0, keepdims=True)
    return jnp.sum(jnp.where(square_column(ROWS), row, 0.0), axis=1, keepdims=True)[:HALF]


def prepare_kernel(mine_ref, theirs_ref, gain_ref, h_ref, upper_ref, lower_ref, power_ref, h, sems):
    pending = fetch(sems, (h_ref, h))
    power = mine_ref[:1, :] + theirs_ref[:1, :]
    power_ref[...] = jnp.broadcast_to(power, (8, ROWS))
    column = jnp.sum(jnp.where(square_column(ROWS), power, 0.0), axis=1, keepdims=True)
    upper_ref[HALF:, :] = tail_of(column[HALF:])
    lower_ref[HALF:, :] = tail_of(column[:HALF])
    pending[0].wait()
    x = normed(h[...], column, gain_ref[...])
    upper_ref[:HALF, :] = x[:HALF]
    lower_ref[:HALF, :] = x[HALF:]


def own_kernel(wq_ref, wk_ref, wv_ref, upper_ref, lower_ref, kv_ref, q_ref, send_ref, wq, wk, wv, sems):
    pending = fetch(sems, (wk_ref, wk), (wv_ref, wv), (wq_ref, wq))
    x = jnp.concatenate([upper_ref[:HALF, :], lower_ref[:HALF, :]], axis=0)
    put_kv(x, wk, wv, kv_ref, send_ref, pending)
    pending[2].wait()
    put_q(x, wq, q_ref, send_ref, 3 * HEAD)


def near_kernel(wk_ref, wv_ref, gain_ref, h1u_ref, x1l_ref, x3u_ref, h3l_ref, x_ref, kv_ref, send_ref, wk, wv, sems):
    pending = fetch(sems, (wk_ref, wk), (wv_ref, wv))
    x_ref[:HALF, :] = normed(h1u_ref[...], power_of(x1l_ref[HALF:, :]), gain_ref[...])
    x_ref[HALF : 2 * HALF, :] = x1l_ref[:HALF, :]
    x_ref[2 * HALF : 3 * HALF, :] = x3u_ref[:HALF, :]
    x_ref[3 * HALF :, :] = normed(h3l_ref[...], power_of(x3u_ref[HALF:, :]), gain_ref[...])
    put_kv(x_ref[...], wk, wv, kv_ref, send_ref, pending)


def far_kernel(wk_ref, wv_ref, gain_ref, power_ref, h2u_ref, h2l_ref, x_ref, kv_ref, send_ref, wk, wv, sems):
    pending = fetch(sems, (wk_ref, wk), (wv_ref, wv))
    column = jnp.sum(jnp.where(square_column(ROWS), power_ref[:1, :], 0.0), axis=1, keepdims=True)
    h = jnp.concatenate([h2u_ref[...], h2l_ref[...]], axis=0)
    x_ref[...] = normed(h, column, gain_ref[...])
    put_kv(x_ref[...], wk, wv, kv_ref, send_ref, pending)


def q_kernel(xa_ref, xb_ref, wq_ref, keep_ref, send_ref):
    for x_ref, s in ((xa_ref, slice(0, 2 * ROWS)), (xb_ref, slice(2 * ROWS, 3 * ROWS))):
        q = jnp.dot(x_ref[...], wq_ref[...], preferred_element_type=f32)
        keep_ref[s, :] = q
        send_ref[s, :] = q.astype(bf16)


def rotated(u, cosine, sine):
    return (u * cosine + pltpu.roll(u, HALF, 1) * sine).astype(bf16)


def rotary_kv_kernel(keep0_ref, got0_ref, keepa_ref, gota_ref, keepb_ref, gotb_ref, cos_ref, sin_ref, kv_ref):
    for keep, got, s in (
        (keep0_ref, got0_ref, slice(0, ROWS)),
        (keepa_ref, gota_ref, slice(ROWS, 3 * ROWS)),
        (keepb_ref, gotb_ref, slice(3 * ROWS, BLOCK)),
    ):
        k = keep[:, HEAD:] + (
            got[:, HEAD : 2 * HEAD].astype(f32) + got[:, 2 * HEAD : 3 * HEAD].astype(f32)
        )
        kv_ref[s, :HEAD] = rotated(k, cos_ref[s, :], sin_ref[s, :])
        kv_ref[s, HEAD:] = (keep[:, :HEAD] + got[:, :HEAD].astype(f32)).astype(bf16)


def rotary_q_kernel(keep0_ref, got0_ref, keep_ref, got_ref, cos_ref, sin_ref, q_ref):
    for keep, got, s, at in (
        (keep0_ref, got0_ref, slice(0, ROWS), 3 * HEAD),
        (keep_ref, got_ref, slice(ROWS, BLOCK), 0),
    ):
        for h in range(HEADS):
            w = slice(h * HEAD, (h + 1) * HEAD)
            u = keep[:, w] + got[:, at + h * HEAD : at + (h + 1) * HEAD].astype(f32)
            q_ref[s, w] = rotated(u, cos_ref[s, :], sin_ref[s, :])


def chunk_of(ref, c):
    at = (0, 1, 3, 2)[c] * ROWS
    return ref[at : at + ROWS, :]


def stacked(q):
    return jnp.concatenate([q[:, h * HEAD : (h + 1) * HEAD] for h in range(HEADS)], axis=0)


def local_kernel(idx_ref, len_ref, q_ref, own_ref, prev_ref, acc_ref, max_ref, sum_ref, bias_ref):
    tc, ctx = idx_ref[0], idx_ref[1]
    lengths = len_ref[...].astype(f32)
    i = lax.broadcasted_iota(jnp.int32, (64, 64), 0)
    j = lax.broadcasted_iota(jnp.int32, (64, 64), 1)
    starts = jnp.sum(jnp.where(i < j, lengths, 0.0), axis=0, keepdims=True)
    prefix = jnp.sum(jnp.where(i[:, :1] < 1, lengths, 0.0), axis=0, keepdims=True).astype(jnp.int32)
    lane = lax.broadcasted_iota(jnp.int32, (ROWS, ROWS), 1)
    for r in range(4):
        a = (tc + r) % 4
        base = ctx * BLOCK + a * ROWS
        pos = base + lax.broadcasted_iota(jnp.int32, (ROWS, 64), 0)
        begun = jnp.where(starts <= pos.astype(f32), starts, 0.0)
        start = jnp.max(begun, axis=1, keepdims=True).astype(jnp.int32)
        t = base + lax.broadcasted_iota(jnp.int32, (ROWS, 1), 0)
        low = jnp.where(start >= prefix, start, jnp.int32(1 << 30))
        keys, values = [], []
        for n in range(5):
            c = (r + n) % 4
            if n == 0:
                chunk = chunk_of(prev_ref, c)
            elif n == 4:
                chunk = chunk_of(own_ref, c)
            else:
                chunk = jnp.where(a + n < 4, chunk_of(prev_ref, c), chunk_of(own_ref, c))
            keys.append(chunk[:, :HEAD])
            values.append(chunk[:, HEAD:])
            u = base + (n - 4) * ROWS + lane
            bias_ref[:, n * ROWS : (n + 1) * ROWS] = jnp.where((u >= low) & (u <= t), 0.0, MASKED)
        keys = jnp.concatenate(keys, axis=0)
        values = jnp.concatenate(values, axis=0)
        q = stacked(chunk_of(q_ref, r))
        s = lax.dot_general(q, keys, (((1,), (1,)), ((), ())), preferred_element_type=f32)
        s = (s.reshape(HEADS, ROWS, 5 * ROWS) + bias_ref[...][None]).reshape(BLOCK, 5 * ROWS)
        largest = jnp.max(s, axis=1, keepdims=True)
        p = jnp.exp2((s - largest) * EXPONENT)
        total = jnp.sum(p, axis=1, keepdims=True)
        acc_ref[r] = jnp.dot(p.astype(bf16), values, preferred_element_type=f32)
        max_ref[r] = jnp.broadcast_to(largest, (BLOCK, HEAD))
        sum_ref[r] = jnp.broadcast_to(total, (BLOCK, HEAD))


def local(idx, lengths, q, own, prev):
    shape = jax.ShapeDtypeStruct((4, BLOCK, HEAD), f32)
    return call(
        local_kernel, "local", [shape] * 3, (idx, lengths, q, own, prev), smem=1,
        scratch=[pltpu.VMEM((ROWS, 5 * ROWS), f32)], vmem=32,
        flops=4 * BLOCK * QW * 640, exps=4 * BLOCK * 640,
    )


def prefix_kernel(chunks, idx_ref, len_ref, acc_ref, max_ref, sum_ref, q_ref, pre_ref, other_ref, wo_ref, *refs):
    bias_ref, attended_ref = refs[-2:]
    tc, ctx = idx_ref[0], idx_ref[1]
    lengths = len_ref[...].astype(f32)
    i = lax.broadcasted_iota(jnp.int32, (64, 1), 0)
    prefix = jnp.sum(jnp.where(i < 1, lengths, 0.0), axis=0, keepdims=True).astype(jnp.int32)
    lane = lax.broadcasted_iota(jnp.int32, (ROWS, ROWS), 1)
    keys, values = [], []
    for c in range(4):
        chunk = chunk_of(pre_ref, c) + chunk_of(other_ref, c)
        keys.append(chunk[:, :HEAD])
        values.append(chunk[:, HEAD:])
    keys = jnp.concatenate(keys, axis=0)
    values = jnp.concatenate(values, axis=0)
    for n, r in enumerate(chunks):
        base = ctx * BLOCK + (tc + r) % 4 * ROWS
        high = jnp.minimum(prefix, base + 1 + lax.broadcasted_iota(jnp.int32, (ROWS, 1), 0))
        for c in range(4):
            u = ((tc + c) % 4) * ROWS + lane
            bias_ref[:, c * ROWS : (c + 1) * ROWS] = jnp.where(u < high, 0.0, MASKED)
        q = stacked(chunk_of(q_ref, r))
        s = lax.dot_general(q, keys, (((1,), (1,)), ((), ())), preferred_element_type=f32)
        s = (s.reshape(HEADS, ROWS, BLOCK) + bias_ref[...][None]).reshape(BLOCK, BLOCK)
        before = max_ref[r][:, :1]
        largest = jnp.maximum(jnp.max(s, axis=1, keepdims=True), before)
        p = jnp.exp2((s - largest) * EXPONENT)
        factor = jnp.exp2((before - largest) * EXPONENT)
        total = jnp.sum(p, axis=1, keepdims=True) + factor * sum_ref[r][:, :1]
        mixed = jnp.dot(p.astype(bf16), values, preferred_element_type=f32) + factor * acc_ref[r]
        mixed = (mixed * (1.0 / total)).astype(bf16)
        for h in range(HEADS):
            attended_ref[n * ROWS : (n + 1) * ROWS, h * HEAD : (h + 1) * HEAD] = mixed[h * ROWS : (h + 1) * ROWS]
    for side, columns in ((0, slice(0, SIDE)), (1, slice(SIDE, 2 * SIDE))):
        out = jnp.dot(attended_ref[...], wo_ref[:, columns], preferred_element_type=f32)
        for n in range(len(chunks)):
            ref = refs[2 * n + side]
            ref[...] = out[n * ROWS : (n + 1) * ROWS].astype(ref.dtype)


def output_kernel(h_ref, *refs):
    for s, (own, one, two) in ((slice(0, SIDE), refs[:3]), (slice(SIDE, 2 * SIDE), refs[3:6])):
        total = own[...] + one[...].astype(f32) + two[...].astype(f32)
        refs[6][:, s] = (h_ref[:, s].astype(f32) + total).astype(bf16)


def finish(chunks, idx, lengths, state, q, pre, wo, kinds):
    n = len(chunks)
    return call(
        functools.partial(prefix_kernel, chunks), "prefix",
        [jax.ShapeDtypeStruct((ROWS, SIDE), kind) for kind in kinds],
        (idx, lengths, *state, q, *pre, wo), smem=1,
        scratch=[pltpu.VMEM((ROWS, BLOCK), f32), pltpu.VMEM((n * ROWS, QW), bf16)],
        flops=n * (4 * ROWS * QW * 512 + 2 * ROWS * QW * 2048), exps=4 * n * ROWS * 512,
    )


def first_kernel(idx_ref, x_ref, a_ref, b_ref, c_ref, out_ref):
    x = jnp.where(idx_ref[1] == 0, x_ref[...], jnp.zeros_like(x_ref))
    out_ref[...] = x + a_ref[...] + b_ref[...] + c_ref[...]


def second_kernel(x_ref, a_ref, b_ref, c_ref, out_ref):
    out_ref[...] = x_ref[...] + a_ref[...] + b_ref[...] + c_ref[...]


FIRST = ((1, 0), (7, 0), (4, 0))
SECOND = (
    {(1, 0): (2, 0), (7, 0): (6, 0), (4, 0): (3, 0), (0, 0): (5, 1)},
    {(1, 0): (2, 1), (7, 0): (6, 1), (4, 0): (5, 0), (0, 0): (3, 1)},
    {(1, 0): (1, 1), (7, 0): (7, 1), (4, 0): (4, 1), (0, 0): (0, 1)},
)


def even_index(chip):
    return 4 * chip[0] + 2 * chip[1]


def spread_far(x, idx):
    got = [lax.ppermute(x, "ctx", [(0, even_index(chip))]) for chip in FIRST]
    at = call(first_kernel, "first", jax.ShapeDtypeStruct(x.shape, x.dtype), (idx, x, *got), smem=1)
    return at, [
        lax.ppermute(at, "ctx", [(even_index(a), even_index(b)) for a, b in step.items()]) for step in SECOND
    ]


def held(*arrays):
    return [pltpu.VMEM(a.shape, a.dtype) for a in arrays] + [pltpu.SemaphoreType.DMA((len(arrays),))]


def per_device(hidden, norm_gain, seg_lengths, wq, wk, wv, wo):
    tc = lax.axis_index("tc")
    ctx = lax.axis_index("ctx")
    idx = jnp.stack([tc, ctx]).astype(jnp.int32)
    def shape(rows, columns, dtype):
        return jax.ShapeDtypeStruct((rows, columns), dtype)

    upper, lower, mine = call(
        squares_kernel, "squares", [shape(HALF, 2048, bf16)] * 2 + [shape(8, ROWS, f32)], (hidden,), stay=(0,),
        scratch=held(hidden),
    )
    h1u = rel(upper, "tc", 4, 1)
    h3l = rel(lower, "tc", 4, 3)
    theirs = rel(mine, "tr", 2, 1)
    gain = norm_gain.reshape(1, -1)
    offset = (jnp.array([0, 1, 3, 2], jnp.int32) + tc) % 4 * ROWS
    positions = (ctx * BLOCK + offset[:, None] + jnp.arange(ROWS, dtype=jnp.int32)[None, :]).reshape(-1)
    frequency = ROPE_BASE ** (-(jnp.arange(HALF, dtype=f32) * 2.0 / HEAD))
    angles = positions.astype(f32)[:, None] * jnp.concatenate([frequency, frequency])[None, :]
    cosine = jnp.cos(angles)
    sine = jnp.sin(angles) * jnp.where(jnp.arange(HEAD) < HALF, -1.0, 1.0)[None, :]
    lengths = seg_lengths.reshape(-1, 1)

    xu, xl, power = call(
        prepare_kernel, "prepare", [shape(TAILED, 2048, bf16)] * 2 + [shape(8, ROWS, f32)], (mine, theirs, gain, hidden), stay=(3,),
        scratch=held(hidden), flops=ROWS * 2048 * 3,
    )
    x1l = rel(xl, "tc", 4, 1)
    x3u = rel(xu, "tc", 4, 3)
    h2u = rel(h1u, "tc", 4, 1)
    h2l = rel(h3l, "tc", 4, 3)
    p2 = rel(power, "tc", 4, 2)
    own_u, _, _ = lax.optimization_barrier((xu, h1u, h3l))
    kv0, q0, send0 = call(
        own_kernel, "own", [shape(ROWS, 2 * HEAD, f32), shape(ROWS, QW, f32), shape(ROWS, 7 * HEAD, bf16)],
        (wq, wk, wv, own_u, xl), stay=(0, 1, 2), scratch=held(wq, wk, wv), flops=2 * ROWS * 2048 * 768,
    )
    got0 = rel(send0, "tr", 2, 1)
    x13, kv13, send13 = call(
        near_kernel, "near",
        [shape(2 * ROWS, 2048, bf16), shape(2 * ROWS, 2 * HEAD, f32), shape(2 * ROWS, 3 * HEAD, bf16)],
        (wk, wv, gain, h1u, x1l, x3u, h3l), stay=(0, 1), scratch=held(wk, wv), flops=4 * ROWS * 2048 * 256,
    )
    got13 = rel(send13, "tr", 2, 1)
    x2, kv2, send2 = call(
        far_kernel, "far",
        [shape(ROWS, 2048, bf16), shape(ROWS, 2 * HEAD, f32), shape(ROWS, 3 * HEAD, bf16)],
        (wk, wv, gain, p2, h2u, h2l), stay=(0, 1), scratch=held(wk, wv), flops=2 * ROWS * 2048 * 256,
    )
    got2 = rel(send2, "tr", 2, 1)
    q1, send_q = call(
        q_kernel, "q", [shape(3 * ROWS, QW, f32), shape(3 * ROWS, QW, bf16)], (x13, x2, wq), flops=6 * ROWS * 2048 * QW,
    )
    got_q = rel(send_q, "tr", 2, 1)
    got2, send_q = lax.optimization_barrier((got2, send_q))
    kv = call(
        rotary_kv_kernel, "rotary_kv", shape(BLOCK, 2 * HEAD, bf16), (kv0, got0, kv13, got13, kv2, got2, cosine, sine),
        flops=BLOCK * 256 * 8,
    )
    prev = lax.ppermute(kv, "ctx", [(i, i + 1) for i in range(lax.axis_size("ctx") - 1)])
    at, got = spread_far(kv, idx)
    q = call(
        rotary_q_kernel, "rotary_q", shape(BLOCK, QW, bf16), (q0, got0, q1, got_q, cosine, sine),
        flops=BLOCK * 512 * 8,
    )
    state = local(idx, lengths, q, kv, prev)
    got, state = lax.optimization_barrier((got, state))
    at = call(second_kernel, "second", shape(BLOCK, 2 * HEAD, bf16), (at, *got))
    pre = (at, lax.ppermute(at, "ctx", [(2 * i, 2 * i + 1) for i in range(lax.axis_size("ctx") // 2)]))
    args = (idx, lengths, state, q, pre, wo)
    left2, right2 = finish((2,), *args, (bf16, bf16))
    left2, right2 = rel(left2, "tc", 4, -1), rel(right2, "tc", 4, 1)
    left1, right1, left3, right3 = finish((1, 3), *args, (f32, bf16, bf16, f32))
    right1, left3 = rel(right1, "tc", 4, -1), rel(left3, "tc", 4, 1)
    left1 = rel((left1 + left2.astype(f32)).astype(bf16), "tc", 4, -1)
    right3 = rel((right3 + right2.astype(f32)).astype(bf16), "tc", 4, 1)
    left0, right0 = finish((0,), *args, (f32, f32))
    return call(
        output_kernel, "output", shape(ROWS, 2048, bf16),
        (hidden, left0, left1, left3, right0, right1, right3), flops=ROWS * 2048 * 3,
    )


def solution(mesh):
    in_specs = (
        P(("ctx", "tc"), "tr"),
        P("tr"),
        P(),
        P("tr", "tc"),
        P("tr", "tc"),
        P("tr", "tc"),
        P("tc", "tr"),
    )
    out_specs = P(("ctx", "tc"), "tr")
    return jax.shard_map(
        per_device, mesh=mesh, in_specs=in_specs, out_specs=out_specs, check_vma=False
    )
```
